32 devices in a mesh: group: 2 (over x), req: 8 (over z, y), chan: 2 (over core).
Axes of the slice: x: 2, y: 2, z: 4, core: 2. Of those that a mesh axis runs over, the one named last changes fastest.
Arguments:
- value_stream: bfloat16 [32, 32, 8192], P(('group', 'req'), None, 'chan'), parts along dimension 0, may hold values from -6 to 6
- gate_stream: bfloat16 [32, 32, 8192], P(('group', 'req'), None, 'chan'), parts along dimension 0, may hold values from -6 to 6
- key_query_stream: bfloat16 [32, 32, 4, 512], P(('group', 'req'), None, 'chan'), parts along dimension 0, may hold values from -6 to 6
- step_stream: bfloat16 [32, 32, 128], P(('group', 'req'), None, 'chan'), parts along dimension 0, may hold values from -6 to 6
- parents: int32 [32, 32], P(('group', 'req')), parts along dimension 0, may hold values from -1 to 30, as said below
- tree_sizes: int32 [32], P(('group', 'req')), parts along dimension 0, may hold values from 1 to 32, as said below
- slot_index: int32 [32], P(('group', 'req')), parts along dimension 0, may hold values from 0 to 15, as said below
- value_cache: bfloat16 [32, 3, 8192], P(('group', 'req'), None, 'chan'), parts along dimension 0, may hold values from -6 to 6
- key_query_cache: bfloat16 [32, 3, 4, 512], P(('group', 'req'), None, 'chan'), parts along dimension 0, may hold values from -6 to 6
- value_conv: bfloat16 [4, 8192], P(None, 'chan'), may hold values from -3 to 3
- key_query_conv: bfloat16 [4, 4, 512], P(None, 'chan'), may hold values from -3 to 3
- step_bias: float32 [128], P('chan'), may hold values from -4 to -1
- log_rate: float32 [128], P('chan'), may hold values from -1 to 2
- skip_gain: float32 [128], P('chan'), may hold values from 0.5 to 1.5
- norm_gain: bfloat16 [8192], P('chan'), may hold values from 0.5 to 1.5
- cached_state: float32 [32, 128, 64, 256], P(('group', 'req'), 'chan'), parts along dimension 0, may hold values from -2 to 2
- out_weight: bfloat16 [8192, 8192], P('chan', 'req'), may hold values from -0.0625 to 0.0625
Outputs:
- layer_out: bfloat16 [32, 32, 8192], P(('group', 'req'), 'chan'), parts along dimension 0
- final_state: float32 [32, 128, 64, 256], P(('group', 'req'), 'chan'), parts along dimension 0
The draws below stay inside these ranges and needn't reach their ends.
There are 2 independent parts, one for each index of `group`. The reference program is written for one: setup_inputs(seed, part) draws one part's arguments, and reference() takes and returns one part's arrays. A program takes and returns all parts, laid end to end along the dimension named above; an argument that names none is the same for every part. Nothing has to cross between parts.
Inputs may be any that keep to these rules, and one draw needn't show every extreme that they name: parents[r, 0] = -1 for the root; for n >= 1, parents[r, n] lies in 0 to n - 1. `tree_sizes`: each size is at least 1; nodes at indices from the size on are padding. The 2 trees of one aligned block of 2 requests hold together at most 48 live nodes, and some block holds exactly 48. `slot_index`: A permutation of the requests that maps each aligned block of 2 requests onto itself.
All inputs are finite; a program needn't handle non-finite values.
Results may differ from the reference program's by a relative error of at most 0.0049.
Values may be sent and summed in bfloat16 or wider, within the bound.
A program may use at most 128 MiB of HBM per device.

```python
import jax
import jax.numpy as jnp
from jax import lax

D = 8192
HEADS = 128
HEAD_DIM = 64
STATE = 256
GROUPS = 4
CONV = 4
NODES = 32
REQ_DEV = 2
REQUESTS = 16
INNER = 8192


def draw_parents(key, part):
    key = jax.random.fold_in(key, 11)
    node_ids = jnp.arange(NODES, dtype=jnp.int32)
    lookback = jax.random.randint(key, (REQUESTS, NODES), 1, 4)
    parent_ids = jnp.maximum(node_ids[None, :] - lookback, 0)
    return jnp.where(node_ids[None, :] == 0, -1, parent_ids).astype(jnp.int32)


def draw_tree_sizes(key, part):
    key = jax.random.fold_in(key, 12)
    total_key, chosen_key, shift_key = jax.random.split(key, 3)
    blocks = REQUESTS // REQ_DEV
    capacity = REQ_DEV * NODES * 3 // 4
    floor_total = REQ_DEV * NODES // 4
    block_total = jax.random.randint(total_key, (blocks,), floor_total, capacity + 1)
    chosen = jax.random.randint(chosen_key, (), 0, blocks)
    full_block = jnp.arange(blocks) == chosen
    block_total = jnp.where(full_block, capacity, block_total)
    position = jnp.arange(REQ_DEV, dtype=jnp.int32)
    tree_size = block_total[:, None] // REQ_DEV + (position[None, :] < block_total[:, None] % REQ_DEV).astype(jnp.int32)
    pair_count = REQ_DEV // 2
    if pair_count > 0:
        left_size = tree_size[:, 0:2 * pair_count:2]
        right_size = tree_size[:, 1:2 * pair_count:2]
        lowest = -jnp.minimum(left_size - 1, NODES - right_size)
        highest_move = jnp.minimum(right_size - 1, NODES - left_size)
        shifted = jax.random.randint(shift_key, left_size.shape, lowest, highest_move + 1)
        first_pair = jnp.arange(pair_count)[None, :] == 0
        shifted = jnp.where(full_block[:, None] & first_pair, NODES - left_size, shifted)
        left_size = left_size + shifted
        right_size = right_size - shifted
        paired = jnp.stack([left_size, right_size], axis=-1).reshape(blocks, 2 * pair_count)
        tree_size = jnp.concatenate([paired, tree_size[:, 2 * pair_count:]], axis=1)
    return tree_size.reshape(-1).astype(jnp.int32)


def draw_slot_index(key, part):
    key = jax.random.fold_in(key, 13)
    blocks = REQUESTS // REQ_DEV
    scores = jax.random.randint(key, (blocks, REQ_DEV), 0, 1 << 20) * REQ_DEV + jnp.arange(REQ_DEV, dtype=jnp.int32)[None, :]
    within = jnp.argsort(scores, axis=1).astype(jnp.int32)
    return (within + jnp.arange(blocks, dtype=jnp.int32)[:, None] * REQ_DEV).reshape(-1).astype(jnp.int32)


def shard_levels(own_key, extent, cuts, least, largest):
    def one(dim, parts):
        heights = jax.random.uniform(jax.random.fold_in(jax.random.fold_in(own_key, 6), dim), (parts,), jnp.float32, least / len(cuts), largest / len(cuts))
        return jnp.repeat(jnp.exp(heights), extent[dim] // parts).reshape((-1,) + (1,) * (len(extent) - dim - 1))

    loudness = one(*cuts[0])
    for cut in cuts[1:]:
        loudness = loudness * one(*cut)
    return loudness


def centred(own_key, extent, width, bound, pieces=(), held_as=jnp.bfloat16):
    values = width * jax.random.normal(own_key, extent, jnp.float32)
    if pieces:
        values = values * shard_levels(own_key, extent, pieces, -0.22, 0.18)
    return jnp.clip(values, -bound, bound).astype(held_as)


def setup_inputs(seed: int = 0, part: int = 0) -> dict:
    seeds = jax.random.split(jax.random.key(seed), 18)
    own_keys = jax.random.split(jax.random.fold_in(seeds[17], part), 18)
    return {
        "value_stream": centred(own_keys[0], (REQUESTS, NODES, INNER), 1.0, 6.0, ((0, 8), (2, 2))),
        "gate_stream": centred(own_keys[1], (REQUESTS, NODES, INNER), 1.0, 6.0, ((0, 8), (2, 2))),
        "key_query_stream": centred(own_keys[2], (REQUESTS, NODES, GROUPS, 2 * STATE), 1.0, 6.0, ((0, 8), (2, 2))),
        "step_stream": centred(own_keys[3], (REQUESTS, NODES, HEADS), 1.0, 6.0, ((0, 8), (2, 2))),
        "parents": draw_parents(jax.random.fold_in(jax.random.fold_in(seeds[17], part), 71), part),
        "tree_sizes": draw_tree_sizes(jax.random.fold_in(jax.random.fold_in(seeds[17], part), 71), part),
        "slot_index": draw_slot_index(jax.random.fold_in(jax.random.fold_in(seeds[17], part), 71), part),
        "value_cache": centred(own_keys[7], (REQUESTS, CONV - 1, INNER), 1.0, 6.0, ((0, 8), (2, 2))),
        "key_query_cache": centred(own_keys[8], (REQUESTS, CONV - 1, GROUPS, 2 * STATE), 1.0, 6.0, ((0, 8), (2, 2))),
        "value_conv": centred(seeds[9], (CONV, INNER), 0.5, 3.0, ((1, 2),)),
        "key_query_conv": centred(seeds[10], (CONV, GROUPS, 2 * STATE), 0.5, 3.0, ((1, 2),)),
        "step_bias": jnp.clip(-4.0 + 3.0 * jax.random.uniform(seeds[11], (HEADS,), jnp.float32) ** shard_levels(seeds[11], (HEADS,), ((0, 2),), -0.2, 0.2), -4.0, -1.0),
        "log_rate": jnp.clip(-1.0 + 3.0 * jax.random.uniform(seeds[12], (HEADS,), jnp.float32) ** shard_levels(seeds[12], (HEADS,), ((0, 2),), -0.2, 0.2), -1.0, 2.0),
        "skip_gain": jnp.clip(0.5 + 1.0 * jax.random.uniform(seeds[13], (HEADS,), jnp.float32) ** shard_levels(seeds[13], (HEADS,), ((0, 2),), -0.2, 0.2), 0.5, 1.5),
        "norm_gain": jnp.clip(1.0 + 0.1 * jax.random.normal(seeds[14], (INNER,), jnp.float32), 0.5, 1.5).astype(jnp.bfloat16),
        "cached_state": centred(own_keys[15], (REQUESTS, HEADS, HEAD_DIM, STATE), 0.3, 2.0, ((0, 8), (1, 2)), jnp.float32),
        "out_weight": centred(seeds[16], (INNER, D), INNER ** -0.5, 0.0625, ((0, 2), (1, 8))),
    }


highest = lax.Precision.HIGHEST
norm_epsilon = 1e-05

def ancestry(parents):
    node_count = parents.shape[-1]
    node_ids = jnp.arange(node_count, dtype=jnp.int32)
    step_one = (parents[:, :, None] == node_ids[None, None, :]).astype(jnp.float32)
    identity_mat = jnp.broadcast_to(jnp.eye(node_count, dtype=jnp.float32), step_one.shape)
    ancestors = identity_mat + step_one
    jump_power = step_one
    reach_span = 2
    while reach_span < node_count:
        jump_power = jnp.einsum('rnj,rjk->rnk', jump_power, jump_power, precision=highest)
        ancestors = jnp.einsum('rnj,rjk->rnk', ancestors, identity_mat + jump_power, precision=highest)
        reach_span = reach_span * 2
    second_power = jnp.einsum('rnj,rjk->rnk', step_one, step_one, precision=highest)
    third_power = jnp.einsum('rnj,rjk->rnk', second_power, step_one, precision=highest)
    return (ancestors, (step_one, second_power, third_power))

def tree_conv(values, cache, weight, shifts, node_depth):
    conv_sum = weight[3].astype(jnp.float32) * values.astype(jnp.float32)
    cache_rows = jnp.arange(3, dtype=jnp.int32)
    for lookback in (1, 2, 3):
        earlier = jnp.einsum('rnj,rjc->rnc', shifts[lookback - 1], values.astype(jnp.float32), precision=highest)
        cache_slot = 3 - lookback + node_depth
        chooser = ((node_depth < lookback)[:, :, None] & (cache_slot[:, :, None] == cache_rows[None, None, :])).astype(jnp.float32)
        earlier = earlier + jnp.einsum('rnq,rqc->rnc', chooser, cache.astype(jnp.float32), precision=highest)
        conv_sum = conv_sum + weight[3 - lookback].astype(jnp.float32) * earlier
    return jax.nn.silu(conv_sum)

def tree_layer(value_rows, gate_rows, kq_rows, step_rows, parents, tree_sizes, value_cache, key_query_cache, value_conv, key_query_conv, step_bias, log_rate, skip_gain, norm_gain, cached_state):
    req_count, node_count, channels = value_rows.shape
    groups = kq_rows.shape[2]
    state_width = kq_rows.shape[3] // 2
    head_count = step_rows.shape[2]
    per_group = head_count // groups
    head_dim = channels // head_count
    ancestors, shifts = ancestry(parents)
    node_depth = (lax.optimization_barrier(jnp.sum(ancestors, axis=-1)) - 1.0).astype(jnp.int32)
    conv_values = tree_conv(value_rows, value_cache, value_conv, shifts, node_depth)
    conv_kq = tree_conv(kq_rows.reshape(req_count, node_count, -1), key_query_cache.reshape(req_count, 3, -1), key_query_conv.reshape(key_query_conv.shape[0], -1), shifts, node_depth)
    conv_kq = conv_kq.reshape(req_count, node_count, groups, 2 * state_width)
    key_rows = conv_kq[..., :state_width]
    queries = conv_kq[..., state_width:]
    step_size = jax.nn.softplus(step_rows.astype(jnp.float32) + step_bias)
    log_level = jnp.einsum('rnj,rjh->rnh', ancestors, step_size * -jnp.exp(log_rate), precision=highest)
    level_gap = log_level[:, :, None, :] - log_level[:, None, :, :]
    path_decay = jnp.exp(jnp.where(ancestors[:, :, :, None] > 0.5, level_gap, -jnp.inf))
    affinity = jnp.einsum('rngs,rjgs->rnjg', queries, key_rows, precision=highest)
    affinity = jnp.repeat(affinity, per_group, axis=3)
    weights = affinity * path_decay * step_size[:, None, :, :]
    values = conv_values.reshape(req_count, node_count, head_count, head_dim)
    inner_out = jnp.einsum('rnjh,rjhp->rnhp', weights, values, precision=highest)
    state_grouped = cached_state.reshape(req_count, groups, per_group, head_dim, state_width)
    carried = jnp.einsum('rngs,rgkps->rngkp', queries, state_grouped, precision=highest)
    carried = carried.reshape(req_count, node_count, head_count, head_dim)
    result = inner_out + carried * jnp.exp(log_level)[..., None] + skip_gain[None, None, :, None] * values
    last_pick = (jnp.arange(node_count)[None, :] == (tree_sizes - 1)[:, None]).astype(jnp.float32)
    last_decay = jnp.einsum('rn,rnjh->rjh', last_pick, path_decay, precision=highest)
    last_level = jnp.einsum('rn,rnh->rh', last_pick, log_level, precision=highest)
    scaled = (values * (last_decay * step_size)[..., None]).reshape(req_count, node_count, groups, per_group, head_dim)
    update = jnp.einsum('rjgkp,rjgs->rgkps', scaled, key_rows, precision=highest).reshape(cached_state.shape)
    final_state = jnp.exp(last_level)[:, :, None, None] * cached_state + update
    gated = result.reshape(req_count, node_count, channels) * jax.nn.silu(gate_rows.astype(jnp.float32))
    blocks = gated.reshape(req_count, node_count, groups, -1)
    inverse_rms = lax.rsqrt(lax.optimization_barrier(jnp.mean(blocks * blocks, axis=-1, keepdims=True)) + norm_epsilon)
    normed = (blocks * inverse_rms).reshape(req_count, node_count, channels) * norm_gain.astype(jnp.float32)
    live_mask = jnp.arange(node_count)[None, :] < tree_sizes[:, None]
    hidden = jnp.where(live_mask[:, :, None], normed, 0.0).astype(jnp.bfloat16)
    return (hidden, final_state)

def reference(value_stream, gate_stream, key_query_stream, step_stream, parents, tree_sizes, slot_index, value_cache, key_query_cache, value_conv, key_query_conv, step_bias, log_rate, skip_gain, norm_gain, cached_state, out_weight):
    hidden, final_state = tree_layer(jnp.take(value_stream, slot_index, axis=0), jnp.take(gate_stream, slot_index, axis=0), jnp.take(key_query_stream, slot_index, axis=0), jnp.take(step_stream, slot_index, axis=0), parents, tree_sizes, value_cache, key_query_cache, value_conv, key_query_conv, step_bias, log_rate, skip_gain, norm_gain, cached_state)
    flat_rows = hidden.reshape(-1, hidden.shape[-1])
    layer_out = jnp.dot(flat_rows, out_weight, preferred_element_type=jnp.float32).astype(jnp.bfloat16)
    return (layer_out.reshape(hidden.shape[0], hidden.shape[1], -1), final_state)
```

```python
import functools

import jax
import jax.numpy as jnp
from jax import lax
from jax.experimental import pallas as pl
from jax.experimental.pallas import tpu as pltpu
from jax.sharding import PartitionSpec as P

f32 = jnp.float32
bf16 = jnp.bfloat16
highest = lax.Precision.HIGHEST
norm_epsilon = 1e-05
MESH = pl.DeviceIdType.MESH
NT = (((1,), (1,)), ((), ()))
TN = (((0,), (0,)), ((), ()))


def iota(shape, dim):
    return lax.broadcasted_iota(jnp.int32, shape, dim)


def dot(a, b):
    return jnp.dot(a, b, preferred_element_type=f32)


def silu(x):
    return x / (1.0 + jnp.exp(-x))


def spread(x, onehot, terms):
    total = None
    for _ in range(terms):
        part = x.astype(bf16)
        x = x - part.astype(f32)
        term = dot(part, onehot)
        total = term if total is None else total + term
    return total


def ssm_kernel(
    slot_s, size_s, parent_s,
    val_ref, gate_ref, kq_ref, step_ref, vcache_ref, kqcache_ref, vw_ref, kqw_ref,
    bias_ref, rate_ref, skip_ref, gain_ref, state_ref,
    hid_ref, unpack_ref, final_ref,
    shift_sc, anc_sc, depth_sc, last_sc, level_sc, size_sc, skip_sc, chan_sc, lane_sc,
):
    g = pl.program_id(0)
    r = pl.program_id(1)
    N = gate_ref.shape[1]
    H = skip_sc.shape[2]
    C = gate_ref.shape[2]
    PD = C // H
    half = N // 2
    slots = [lax.rem(slot_s[k], 2) for k in range(2)]

    @pl.when((g == 0) & (r == 0))
    def _():
        M = 2 * N
        rows, cols = iota((M, M), 0), iota((M, M), 1)
        par = jnp.full((M, M), -1, jnp.int32)
        for k in range(2):
            for n in range(1, N):
                par = jnp.where(rows == k * N + n, parent_s[k, n] + k * N, par)
        one = jnp.where(par == cols, 1.0, 0.0).astype(f32)
        eye = jnp.where(rows == cols, 1.0, 0.0).astype(f32)
        step_b = one.astype(bf16)
        second = dot(step_b, step_b)
        third = dot(second.astype(bf16), step_b)
        anc = eye + one
        power = second
        reach = 2
        while reach < N:
            anc = dot(anc.astype(bf16), (eye + power).astype(bf16))
            reach *= 2
            if reach < N:
                power = dot(power.astype(bf16), power.astype(bf16))
        for k in range(2):
            lo, hi = k * N, (k + 1) * N
            for i, mat in enumerate((one, second, third)):
                tile = jnp.where(
                    iota((M, N), 0) - iota((M, N), 1) == lo, 1.0, 0.0
                ).astype(bf16)
                shift_sc[k, i * N:(i + 1) * N, :] = dot(mat[lo:hi].astype(bf16), tile).astype(bf16)
        fold = jnp.where(lax.rem(iota((M, 4 * N), 0), N) == lax.rem(iota((M, 4 * N), 1), N), 1.0, 0.0)
        anc_sc[...] = dot(anc.astype(bf16), fold.astype(bf16))
        depth_sc[...] = jnp.broadcast_to(jnp.sum(anc, axis=1, keepdims=True) - 1.0, depth_sc.shape)
        row_h = iota((M, H), 0)
        pick = (row_h == size_s[0] - 1) | (row_h == N + size_s[1] - 1)
        last_sc[...] = lax.dot_general(
            anc.astype(bf16), jnp.where(pick, 1.0, 0.0).astype(bf16), TN, preferred_element_type=f32
        )
        x = jnp.concatenate([step_ref[slots[0]], step_ref[slots[1]]], axis=0).astype(f32) + bias_ref[...]
        step = jnp.maximum(x, 0.0) + jnp.log1p(jnp.exp(-jnp.abs(x)))
        rate = -jnp.exp(rate_ref[...])
        level = jnp.dot(anc, step * rate, precision=highest, preferred_element_type=f32)
        for k in range(2):
            level_sc[k] = level[:, k * H:(k + 1) * H]
            size_sc[k] = step[:, k * H:(k + 1) * H]
            skip_sc[k] = jnp.broadcast_to(skip_ref[:, k * H:(k + 1) * H], skip_sc.shape[1:])
        chan_sc[...] = jnp.where(iota((H, C), 1) // PD == iota((H, C), 0), 1.0, 0.0).astype(bf16)
        lane_sc[...] = jnp.where(iota((H, H * N), 1) // N == iota((H, H * N), 0), 1.0, 0.0).astype(bf16)
        u_row, u_col = iota((N, half), 0), iota((N, half), 1)
        req = u_row // half
        node = u_row - req * half
        over = jnp.maximum(size_s[0] - half, 0)
        place = node + jnp.where(req == 1, over, 0)
        live = node + half < jnp.where(req == 1, size_s[1], size_s[0])
        unpack_ref[...] = jnp.where((u_col == place) & live, 1.0, 0.0).astype(bf16)

    slot = lax.rem(slot_s[r], 2)
    own = pl.ds(pl.multiple_of(r * N, N), N)
    depth = depth_sc[own, 0:1]
    shifts = shift_sc[r]

    def conv(x, cache, w):
        w = w.astype(f32)
        cache = cache.astype(f32)
        back = dot(shifts, x)
        total = w[3:4] * x.astype(f32)
        for k in range(1, 4):
            total = total + w[3 - k:4 - k] * back[(k - 1) * N:k * N]
        c0, c1, c2 = cache[0:1], cache[1:2], cache[2:3]
        w0, w1, w2 = w[0:1], w[1:2], w[2:3]
        total = total + jnp.where(depth == 0.0, w2 * c2 + w1 * c1 + w0 * c0, 0.0)
        total = total + jnp.where(depth == 1.0, w1 * c2 + w0 * c1, 0.0)
        total = total + jnp.where(depth == 2.0, w0 * c2, 0.0)
        return silu(total)

    kq = conv(kq_ref[slot], kqcache_ref[r], kqw_ref[...])
    S = kq.shape[1] // 2
    key, query = kq[:, :S], kq[:, S:]
    key_b, query_b = key.astype(bf16), query.astype(bf16)
    level = level_sc[g, own, :]
    step = size_sc[g, own, :]
    m = size_s[r] - 1
    level_m = jnp.sum(jnp.where(iota((N, H), 0) == m, level, 0.0), axis=0, keepdims=True)
    last_decay = jnp.exp(jnp.where(last_sc[own, :] > 0.5, level_m - level, -1e30))
    decay_m = jnp.exp(level_m)
    stacked = jnp.concatenate([step, jnp.exp(level), last_decay, skip_sc[g]], axis=0)
    wide = spread(stacked, chan_sc[...], 2)
    level_x = spread(level, lane_sc[...], 3)
    diag = lax.rem(iota((N, H * N), 1), N) == iota((N, H * N), 0)
    level_row = jnp.sum(jnp.where(diag, level_x, 0.0), axis=0, keepdims=True)
    anc4 = anc_sc[own, :] > 0.5
    key4 = jnp.concatenate([key] * 4, axis=0)
    affinity4 = lax.dot_general(query, key4, NT, precision=highest, preferred_element_type=f32)
    block_mask = iota((4 * N, 4 * PD), 0) // N == iota((4 * N, 4 * PD), 1) // PD

    pieces = []
    for q in range(H // 4):
        cs = slice(q * 4 * PD, (q + 1) * 4 * PD)
        ls = slice(q * 4 * N, (q + 1) * 4 * N)
        values = conv(val_ref[slot, :, cs], vcache_ref[r, :, cs], vw_ref[:, cs])
        gap = level_x[:, ls] - level_row[:, ls]
        weights = affinity4 * jnp.exp(jnp.where(anc4, gap, -1e30))
        stepped = values * wide[0:N, cs]
        four = jnp.concatenate([stepped] * 4, axis=0)
        four = jnp.where(block_mask, four, 0.0).astype(bf16)
        inner = dot(weights.astype(bf16), four)
        state = state_ref[0, 4 * q:4 * q + 4].reshape(4 * PD, S)
        carried = lax.dot_general(query_b, state.astype(bf16), NT, preferred_element_type=f32)
        result = inner + carried * wide[N:2 * N, cs] + wide[3 * N:3 * N + 1, cs] * values
        pieces.append(result * silu(gate_ref[slot, :, cs].astype(f32)))
        scaled = (stepped * wide[2 * N:3 * N, cs]).astype(bf16)
        update = lax.dot_general(scaled, key_b, TN, preferred_element_type=f32)
        for k in range(4):
            h = 4 * q + k
            final_ref[0, h] = (
                jnp.broadcast_to(decay_m[:, h:h + 1], (PD, S)) * state_ref[0, h]
                + update[k * PD:(k + 1) * PD]
            )
    square = sum(jnp.sum(p * p, axis=1, keepdims=True) for p in pieces)
    inverse = lax.rsqrt(square / C + norm_epsilon)
    live = iota((N, 1), 0) < size_s[r]
    a_row, a_col = iota((half, half), 0), iota((half, half), 1)
    over = jnp.where(r == 1, jnp.maximum(size_s[0] - half, 0), 0)
    pack = jnp.where(a_row == a_col + over, 1.0, 0.0).astype(bf16)
    for q, piece in enumerate(pieces):
        cs = slice(q * 4 * PD, (q + 1) * 4 * PD)
        normed = piece * inverse * gain_ref[:, cs].astype(f32)
        hidden = jnp.where(live, normed, 0.0).astype(bf16)
        hid_ref[0, pl.ds(pl.multiple_of(r * half, half), half), cs] = hidden[:half]
        tail = dot(pack, hidden[half:])

        @pl.when(r == 0)
        def _():
            hid_ref[0, N:, cs] = tail.astype(bf16)

        @pl.when(r == 1)
        def _():
            hid_ref[0, N:, cs] = (hid_ref[0, N:, cs].astype(f32) + tail).astype(bf16)


def comm_kernel(
    R, packed, unpack, w_any, out,
    wbuf, gath, part, other, fin, back,
    w_sem, send_sem, recv_sem, ex_send, ex_recv, home_send, home_recv,
):
    gi, me, c = lax.axis_index("group"), lax.axis_index("req"), lax.axis_index("chan")
    A = R // 2
    a = me // 2
    b = me - 2 * a
    pair = 2 * a + 1 - b
    cols = wbuf.shape[1]
    rows = gath.shape[2]
    low = out.shape[1] * 2
    wcopy = pltpu.make_async_copy(w_any, wbuf, w_sem)
    wcopy.start()

    barrier = pltpu.get_barrier_semaphore()
    for k in range(1, R):
        pl.semaphore_signal(barrier, inc=1, device_id=(gi, lax.rem(me + k, R), c), device_id_type=MESH)
    pl.semaphore_signal(barrier, inc=1, device_id=(gi, me, 1 - c), device_id_type=MESH)
    pl.semaphore_wait(barrier, R)

    def push(src, way, slot, u, target):
        return pltpu.make_async_remote_copy(
            src_ref=src, dst_ref=gath.at[slot, u],
            send_sem=send_sem.at[way, slot, u], recv_sem=recv_sem.at[slot, u],
            device_id=(gi, target, c), device_id_type=MESH,
        )

    def arrived(slot, u):
        push(gath.at[slot, u], 0, slot, u, pair).wait_recv()

    def exchange(slot, lo, hi):
        return pltpu.make_async_remote_copy(
            src_ref=part.at[slot, lo:hi], dst_ref=other.at[slot, lo:hi],
            send_sem=ex_send.at[slot], recv_sem=ex_recv.at[slot],
            device_id=(gi, me, 1 - c), device_id_type=MESH,
        )

    def home(slot, place, target, lo, hi):
        return pltpu.make_async_remote_copy(
            src_ref=fin.at[slot, lo:hi], dst_ref=back.at[place, lo:hi],
            send_sem=home_send.at[slot], recv_sem=home_recv.at[place],
            device_id=(gi, target, c), device_id_type=MESH,
        )

    def by_core(fn):
        @pl.when(c == 0)
        def _():
            fn((0, low), (low, rows))

        @pl.when(c == 1)
        def _():
            fn((low, rows), (0, low))

    depth = gath.shape[3]

    def multiply(slot, first, second):
        @pl.loop(0, cols // 256)
        def _(t):
            at = pl.ds(pl.multiple_of(t * 256, 256), 256)
            part[slot, :, at] = dot(first[...], wbuf[:depth, at]) + dot(second[...], wbuf[depth:, at])
        by_core(lambda mine, theirs: exchange(slot, *theirs).start())

    def finish(slot):
        def fn(mine, theirs):
            exchange(slot, *mine).wait_recv()
            at = slice(*mine)
            fin[slot, at] = (part[slot, at] + other[slot, at]).astype(bf16)
            home(slot, me, slot, *mine).start()
        by_core(fn)

    for u in range(2):
        @pl.when(a < A - 1)
        def _():
            push(packed.at[u], 0, me, u, me + 2).start()

        @pl.when(a > 0)
        def _():
            push(packed.at[u], 1, me, u, me - 2).start()
        push(packed.at[u], 2, me, u, pair).start()

    wcopy.wait()
    multiply(me, packed.at[0], packed.at[1])

    def finish_own(mine, theirs):
        exchange(me, *mine).wait_recv()
        at = slice(*mine)
        back[me, at] = (part[me, at] + other[me, at]).astype(bf16)
    by_core(finish_own)

    def step(t, carry):
        left, right = a - t, a + t
        pleft, pright = a - t + 1, a + t - 1
        for u in range(2):
            @pl.when(left >= 0)
            def _():
                s = 2 * left + b
                arrived(s, u)

                @pl.when(a < A - 1)
                def _():
                    push(gath.at[s, u], 0, s, u, me + 2).start()
                push(gath.at[s, u], 2, s, u, pair).start()

            @pl.when(right < A)
            def _():
                s = 2 * right + b
                arrived(s, u)

                @pl.when(a > 0)
                def _():
                    push(gath.at[s, u], 1, s, u, me - 2).start()
                push(gath.at[s, u], 2, s, u, pair).start()
        work = (
            (left >= 0, 2 * left + b, False),
            (right < A, 2 * right + b, False),
            (pleft >= 0, 2 * pleft + 1 - b, True),
            ((pright < A) & (t > 1), 2 * pright + 1 - b, True),
        )
        for valid, s, wait in work:
            @pl.when(valid)
            def _():
                if wait:
                    arrived(s, 0)
                    arrived(s, 1)
                multiply(s, gath.at[s, 0], gath.at[s, 1])
        for valid, s, wait in work:
            @pl.when(valid)
            def _():
                finish(s)
        return carry

    lax.fori_loop(1, A + 1, step, 0)

    def place(s, carry):
        at = pl.ds(pl.multiple_of(s * cols, cols), cols)

        def wait(mine, theirs):
            @pl.when(s != me)
            def _():
                home(s, s, s, *mine).wait_recv()
        by_core(wait)

        @pl.when(c == 0)
        def _():
            out[0, :, at] = back[s, :low // 2]
            out[1, :, at] = back[s, low // 2:low]

        @pl.when(c == 1)
        def _():
            both = dot(unpack[...], back[s, low:]).astype(bf16)
            out[0, :, at] = both[:low // 2]
            out[1, :, at] = both[low // 2:]
        return carry

    lax.fori_loop(0, R, place, 0)

    def drain(s, carry):
        sa = s // 2
        mine_col = s - 2 * sa == b

        def fn(mine, theirs):
            exchange(s, *theirs).wait_send()

            @pl.when(s != me)
            def _():
                home(s, me, s, *mine).wait_send()
        by_core(fn)
        for u in range(2):
            @pl.when(mine_col & (sa <= a) & (a < A - 1))
            def _():
                push(packed.at[u], 0, s, u, me + 2).wait_send()

            @pl.when(mine_col & (sa >= a) & (a > 0))
            def _():
                push(packed.at[u], 1, s, u, me - 2).wait_send()

            @pl.when(mine_col)
            def _():
                push(packed.at[u], 2, s, u, pair).wait_send()
        return carry

    lax.fori_loop(0, R, drain, 0)


def local(
    value_stream, gate_stream, key_query_stream, step_stream, parents, tree_sizes, slot_index,
    value_cache, key_query_cache, value_conv, key_query_conv, step_bias, log_rate, skip_gain,
    norm_gain, cached_state, out_weight,
):
    Q, N, C = value_stream.shape
    G = key_query_stream.shape[2]
    heads, PD, S = cached_state.shape[1:]
    H = heads // G
    CG = C // G
    R = lax.axis_size("req")
    packed_rows = N + N // 2
    kq = key_query_stream.reshape(Q, N, -1)
    kq_cache = key_query_cache.reshape(Q, 3, -1)
    kq_conv = key_query_conv.reshape(key_query_conv.shape[0], -1)
    smem = pl.BlockSpec(memory_space=pltpu.SMEM)
    whole = lambda x: pl.BlockSpec(x.shape, lambda g, r: (0,) * x.ndim)
    by_group = lambda x, n: pl.BlockSpec(x.shape[:-1] + (n,), lambda g, r: (0,) * (x.ndim - 1) + (g,))
    bias, rate, skip = (x.reshape(1, -1) for x in (step_bias, log_rate, skip_gain))
    gain = norm_gain.reshape(1, -1)
    state_spec = pl.BlockSpec((1, H, PD, S), lambda g, r: (r, g, 0, 0))
    packed, unpack, final_state = pl.pallas_call(
        ssm_kernel,
        grid=(G, Q),
        out_shape=(
            jax.ShapeDtypeStruct((G, packed_rows, CG), bf16),
            jax.ShapeDtypeStruct((N, N // 2), bf16),
            jax.ShapeDtypeStruct(cached_state.shape, f32),
        ),
        in_specs=[
            smem, smem, smem,
            by_group(value_stream, CG), by_group(gate_stream, CG), by_group(kq, 2 * S), whole(step_stream),
            by_group(value_cache, CG), by_group(kq_cache, 2 * S), by_group(value_conv, CG),
            by_group(kq_conv, 2 * S), whole(bias), whole(rate), whole(skip), by_group(gain, CG), state_spec,
        ],
        out_specs=(
            pl.BlockSpec((1, packed_rows, CG), lambda g, r: (g, 0, 0)),
            pl.BlockSpec((N, N // 2), lambda g, r: (0, 0)),
            state_spec,
        ),
        scratch_shapes=[
            pltpu.VMEM((2, 3 * N, N), bf16),
            pltpu.VMEM((2 * N, 4 * N), f32),
            pltpu.VMEM((2 * N, 128), f32),
            pltpu.VMEM((2 * N, H), f32),
            pltpu.VMEM((2, 2 * N, H), f32),
            pltpu.VMEM((2, 2 * N, H), f32),
            pltpu.VMEM((2, 8, H), f32),
            pltpu.VMEM((H, CG), bf16),
            pltpu.VMEM((H, H * N), bf16),
        ],
        compiler_params=pltpu.CompilerParams(vmem_limit_bytes=40 * 2**20),
        name="ssm",
    )(
        slot_index, tree_sizes, parents, value_stream, gate_stream, kq, step_stream, value_cache,
        kq_cache, value_conv, kq_conv, bias, rate, skip, gain, cached_state,
    )
    cols = out_weight.shape[1]
    vmem = pl.BlockSpec(memory_space=pltpu.VMEM)
    dma = pltpu.SemaphoreType.DMA
    out = pl.pallas_call(
        functools.partial(comm_kernel, R),
        out_shape=jax.ShapeDtypeStruct((Q, N // 2, R * cols), bf16),
        in_specs=[vmem, vmem, pl.BlockSpec(memory_space=pl.ANY)],
        out_specs=vmem,
        scratch_shapes=[
            pltpu.VMEM(out_weight.shape, bf16),
            pltpu.VMEM((R, G, packed_rows, CG), bf16),
            pltpu.VMEM((R, packed_rows, cols), f32),
            pltpu.VMEM((R, packed_rows, cols), f32),
            pltpu.VMEM((R, packed_rows, cols), bf16),
            pltpu.VMEM((R, packed_rows, cols), bf16),
            dma, dma((3, R, G)), dma((R, G)), dma((R,)), dma((R,)), dma((R,)), dma((R,)),
        ],
        compiler_params=pltpu.CompilerParams(
            collective_id=0, has_side_effects=True, vmem_limit_bytes=40 * 2**20
        ),
        name="project",
    )(packed, unpack, out_weight)
    return (out, final_state)


def solution(mesh):
    return jax.shard_map(
        local,
        mesh=mesh,
        in_specs=(
            P(("group", "req"), None, "chan"),
            P(("group", "req"), None, "chan"),
            P(("group", "req"), None, "chan", None),
            P(("group", "req"), None, "chan"),
            P(("group", "req"), None),
            P(("group", "req")),
            P(("group", "req")),
            P(("group", "req"), None, "chan"),
            P(("group", "req"), None, "chan", None),
            P(None, "chan"),
            P(None, "chan", None),
            P("chan"),
            P("chan"),
            P("chan"),
            P("chan"),
            P(("group", "req"), "chan", None, None),
            P("chan", "req"),
        ),
        out_specs=(P(("group", "req"), "chan", None), P(("group", "req"), "chan", None, None)),
        check_vma=False,
    )
```

```python
import functools

import jax
import jax.numpy as jnp
from jax import lax
from jax.experimental import pallas as pl
from jax.experimental.pallas import tpu as pltpu
from jax.sharding import PartitionSpec as P

f32 = jnp.float32
bf16 = jnp.bfloat16
highest = lax.Precision.HIGHEST
norm_epsilon = 1e-05
MESH = pl.DeviceIdType.MESH
NT = (((1,), (1,)), ((), ()))
TN = (((0,), (0,)), ((), ()))


def iota(shape, dim):
    return lax.broadcasted_iota(jnp.int32, shape, dim)


def dot(a, b):
    return jnp.dot(a, b, preferred_element_type=f32)


def silu(x):
    return x / (1.0 + jnp.exp(-x))


def spread(x, onehot, terms):
    total = None
    for _ in range(terms):
        part = x.astype(bf16)
        x = x - part.astype(f32)
        term = dot(part, onehot)
        total = term if total is None else total + term
    return total


def ssm_kernel(
    slot_s, size_s, parent_s,
    val_ref, gate_ref, kq_ref, step_ref, vcache_ref, kqcache_ref, vw_ref, kqw_ref,
    bias_ref, rate_ref, skip_ref, gain_ref, state_ref,
    hid_ref, unpack_ref, final_ref,
    shift_sc, anc_sc, depth_sc, last_sc, level_sc, size_sc, skip_sc, chan_sc, lane_sc,
):
    g = pl.program_id(0)
    r = pl.program_id(1)
    N = gate_ref.shape[1]
    H = skip_sc.shape[2]
    C = gate_ref.shape[2]
    PD = C // H
    half = N // 2
    slots = [lax.rem(slot_s[k], 2) for k in range(2)]

    @pl.when((g == 0) & (r == 0))
    def _():
        M = 2 * N
        rows, cols = iota((M, M), 0), iota((M, M), 1)
        par = jnp.full((M, M), -1, jnp.int32)
        for k in range(2):
            for n in range(1, N):
                par = jnp.where(rows == k * N + n, parent_s[k, n] + k * N, par)
        one = jnp.where(par == cols, 1.0, 0.0).astype(f32)
        eye = jnp.where(rows == cols, 1.0, 0.0).astype(f32)
        step_b = one.astype(bf16)
        second = dot(step_b, step_b)
        third = dot(second.astype(bf16), step_b)
        anc = eye + one
        power = second
        reach = 2
        while reach < N:
            anc = dot(anc.astype(bf16), (eye + power).astype(bf16))
            reach *= 2
            if reach < N:
                power = dot(power.astype(bf16), power.astype(bf16))
        for k in range(2):
            lo, hi = k * N, (k + 1) * N
            for i, mat in enumerate((one, second, third)):
                tile = jnp.where(
                    iota((M, N), 0) - iota((M, N), 1) == lo, 1.0, 0.0
                ).astype(bf16)
                shift_sc[k, i * N:(i + 1) * N, :] = dot(mat[lo:hi].astype(bf16), tile).astype(bf16)
        fold = jnp.where(lax.rem(iota((M, 4 * N), 0), N) == lax.rem(iota((M, 4 * N), 1), N), 1.0, 0.0)
        anc_sc[...] = dot(anc.astype(bf16), fold.astype(bf16))
        depth_sc[...] = jnp.broadcast_to(jnp.sum(anc, axis=1, keepdims=True) - 1.0, depth_sc.shape)
        row_h = iota((M, H), 0)
        pick = (row_h == size_s[0] - 1) | (row_h == N + size_s[1] - 1)
        last_sc[...] = lax.dot_general(
            anc.astype(bf16), jnp.where(pick, 1.0, 0.0).astype(bf16), TN, preferred_element_type=f32
        )
        x = jnp.concatenate([step_ref[slots[0]], step_ref[slots[1]]], axis=0).astype(f32) + bias_ref[...]
        step = jnp.maximum(x, 0.0) + jnp.log1p(jnp.exp(-jnp.abs(x)))
        rate = -jnp.exp(rate_ref[...])
        level = jnp.dot(anc, step * rate, precision=highest, preferred_element_type=f32)
        for k in range(2):
            level_sc[k] = level[:, k * H:(k + 1) * H]
            size_sc[k] = step[:, k * H:(k + 1) * H]
            skip_sc[k] = jnp.broadcast_to(skip_ref[:, k * H:(k + 1) * H], skip_sc.shape[1:])
        chan_sc[...] = jnp.where(iota((H, C), 1) // PD == iota((H, C), 0), 1.0, 0.0).astype(bf16)
        lane_sc[...] = jnp.where(iota((H, H * N), 1) // N == iota((H, H * N), 0), 1.0, 0.0).astype(bf16)
        u_row, u_col = iota((N, half), 0), iota((N, half), 1)
        req = u_row // half
        node = u_row - req * half
        over = jnp.maximum(size_s[0] - half, 0)
        place = node + jnp.where(req == 1, over, 0)
        live = node + half < jnp.where(req == 1, size_s[1], size_s[0])
        unpack_ref[...] = jnp.where((u_col == place) & live, 1.0, 0.0).astype(bf16)

    slot = lax.rem(slot_s[r], 2)
    own = pl.ds(pl.multiple_of(r * N, N), N)
    depth = depth_sc[own, 0:1]
    shifts = shift_sc[r]

    def conv(x, cache, w):
        back = dot(shifts, x)
        c0, c1, c2 = cache
        w0, w1, w2, w3 = w
        total = w3 * x.astype(f32)
        for k in range(1, 4):
            total = total + w[3 - k] * back[(k - 1) * N:k * N]
        total = total + jnp.where(depth == 0.0, w2 * c2 + w1 * c1 + w0 * c0, 0.0)
        total = total + jnp.where(depth == 1.0, w1 * c2 + w0 * c1, 0.0)
        total = total + jnp.where(depth == 2.0, w0 * c2, 0.0)
        return silu(total)

    def row_of(pair, index):
        pair = pair.astype(f32)
        return jnp.where(index == 0, pair[0:1], pair[1:2])

    kq_rows = jnp.where(g == 0, kq_ref[slot, :, 0, :].astype(f32), kq_ref[slot, :, 1, :].astype(f32))
    kq = conv(
        kq_rows.astype(bf16),
        [row_of(kqcache_ref[r, k], g) for k in range(3)],
        [row_of(kqw_ref[k], g) for k in range(4)],
    )
    S = kq.shape[1] // 2
    key, query = kq[:, :S], kq[:, S:]
    key_b, query_b = key.astype(bf16), query.astype(bf16)
    level = level_sc[g, own, :]
    step = size_sc[g, own, :]
    m = size_s[r] - 1
    level_m = jnp.sum(jnp.where(iota((N, H), 0) == m, level, 0.0), axis=0, keepdims=True)
    last_decay = jnp.exp(jnp.where(last_sc[own, :] > 0.5, level_m - level, -1e30))
    decay_m = jnp.exp(level_m)
    stacked = jnp.concatenate([step, jnp.exp(level), last_decay, skip_sc[g]], axis=0)
    wide = spread(stacked, chan_sc[...], 2)
    level_x = spread(level, lane_sc[...], 3)
    diag = lax.rem(iota((N, H * N), 1), N) == iota((N, H * N), 0)
    level_row = jnp.sum(jnp.where(diag, level_x, 0.0), axis=0, keepdims=True)
    anc4 = anc_sc[own, :] > 0.5
    key4 = jnp.concatenate([key] * 4, axis=0)
    affinity4 = lax.dot_general(query, key4, NT, precision=highest, preferred_element_type=f32)
    block_mask = iota((4 * N, 4 * PD), 0) // N == iota((4 * N, 4 * PD), 1) // PD

    pieces = []
    for q in range(H // 4):
        cs = slice(q * 4 * PD, (q + 1) * 4 * PD)
        ls = slice(q * 4 * N, (q + 1) * 4 * N)
        taps = vw_ref[:, cs].astype(f32)
        values = conv(
            val_ref[slot, :, cs],
            [row_of(vcache_ref[k, :, cs], r) for k in range(3)],
            [taps[k:k + 1] for k in range(4)],
        )
        gap = level_x[:, ls] - level_row[:, ls]
        weights = affinity4 * jnp.exp(jnp.where(anc4, gap, -1e30))
        stepped = values * wide[0:N, cs]
        four = jnp.concatenate([stepped] * 4, axis=0)
        four = jnp.where(block_mask, four, 0.0).astype(bf16)
        inner = dot(weights.astype(bf16), four)
        state = state_ref[0, 4 * q:4 * q + 4].reshape(4 * PD, S)
        carried = lax.dot_general(query_b, state.astype(bf16), NT, preferred_element_type=f32)
        result = inner + carried * wide[N:2 * N, cs] + wide[3 * N:3 * N + 1, cs] * values
        pieces.append(result * silu(gate_ref[slot, :, cs].astype(f32)))
        scaled = (stepped * wide[2 * N:3 * N, cs]).astype(bf16)
        update = lax.dot_general(scaled, key_b, TN, preferred_element_type=f32)
        for k in range(4):
            h = 4 * q + k
            final_ref[0, h] = (
                jnp.broadcast_to(decay_m[:, h:h + 1], (PD, S)) * state_ref[0, h]
                + update[k * PD:(k + 1) * PD]
            )
    square = sum(jnp.sum(p * p, axis=1, keepdims=True) for p in pieces)
    inverse = lax.rsqrt(square / C + norm_epsilon)
    live = iota((N, 1), 0) < size_s[r]
    a_row, a_col = iota((half, half), 0), iota((half, half), 1)
    over = jnp.where(r == 1, jnp.maximum(size_s[0] - half, 0), 0)
    pack = jnp.where(a_row == a_col + over, 1.0, 0.0).astype(bf16)
    for q, piece in enumerate(pieces):
        cs = slice(q * 4 * PD, (q + 1) * 4 * PD)
        normed = piece * inverse * gain_ref[cs].astype(f32).reshape(1, -1)
        hidden = jnp.where(live, normed, 0.0).astype(bf16)
        hid_ref[0, pl.ds(pl.multiple_of(r * half, half), half), cs] = hidden[:half]
        tail = dot(pack, hidden[half:])

        @pl.when(r == 0)
        def _():
            hid_ref[0, N:, cs] = tail.astype(bf16)

        @pl.when(r == 1)
        def _():
            hid_ref[0, N:, cs] = (hid_ref[0, N:, cs].astype(f32) + tail).astype(bf16)


def comm_kernel(
    R, packed, unpack, w_any, out,
    wbuf, gath, part, other, fin, back,
    w_sem, send_sem, recv_sem, ex_send, ex_recv, home_send, home_recv,
):
    gi, me, c = lax.axis_index("group"), lax.axis_index("req"), lax.axis_index("chan")
    A = R // 2
    a = me // 2
    b = me - 2 * a
    pair = 2 * a + 1 - b
    cols = wbuf.shape[1]
    rows = gath.shape[2]
    low = out.shape[1] * 2
    wcopy = pltpu.make_async_copy(w_any, wbuf, w_sem)
    wcopy.start()

    barrier = pltpu.get_barrier_semaphore()
    for k in range(1, R):
        pl.semaphore_signal(barrier, inc=1, device_id=(gi, lax.rem(me + k, R), c), device_id_type=MESH)
    pl.semaphore_signal(barrier, inc=1, device_id=(gi, me, 1 - c), device_id_type=MESH)
    pl.semaphore_wait(barrier, R)

    def push(src, way, slot, u, target):
        return pltpu.make_async_remote_copy(
            src_ref=src, dst_ref=gath.at[slot, u],
            send_sem=send_sem.at[way, slot, u], recv_sem=recv_sem.at[slot, u],
            device_id=(gi, target, c), device_id_type=MESH,
        )

    def arrived(slot, u):
        push(gath.at[slot, u], 0, slot, u, pair).wait_recv()

    def exchange(slot, lo, hi):
        return pltpu.make_async_remote_copy(
            src_ref=part.at[slot, lo:hi], dst_ref=other.at[slot, lo:hi],
            send_sem=ex_send.at[slot], recv_sem=ex_recv.at[slot],
            device_id=(gi, me, 1 - c), device_id_type=MESH,
        )

    def home(slot, place, target, lo, hi):
        return pltpu.make_async_remote_copy(
            src_ref=fin.at[slot, lo:hi], dst_ref=back.at[place, lo:hi],
            send_sem=home_send.at[slot], recv_sem=home_recv.at[place],
            device_id=(gi, target, c), device_id_type=MESH,
        )

    def by_core(fn):
        @pl.when(c == 0)
        def _():
            fn((0, low), (low, rows))

        @pl.when(c == 1)
        def _():
            fn((low, rows), (0, low))

    depth = gath.shape[3]

    def multiply(slot, first, second):
        @pl.loop(0, cols // 256)
        def _(t):
            at = pl.ds(pl.multiple_of(t * 256, 256), 256)
            part[slot, :, at] = dot(first[...], wbuf[:depth, at]) + dot(second[...], wbuf[depth:, at])
        by_core(lambda mine, theirs: exchange(slot, *theirs).start())

    def finish(slot):
        def fn(mine, theirs):
            exchange(slot, *mine).wait_recv()
            at = slice(*mine)
            fin[slot, at] = (part[slot, at] + other[slot, at]).astype(bf16)
            home(slot, me, slot, *mine).start()
        by_core(fn)

    for u in range(2):
        @pl.when(a < A - 1)
        def _():
            push(packed.at[u], 0, me, u, me + 2).start()

        @pl.when(a > 0)
        def _():
            push(packed.at[u], 1, me, u, me - 2).start()
        push(packed.at[u], 2, me, u, pair).start()

    wcopy.wait()
    multiply(me, packed.at[0], packed.at[1])

    def finish_own(mine, theirs):
        exchange(me, *mine).wait_recv()
        at = slice(*mine)
        back[me, at] = (part[me, at] + other[me, at]).astype(bf16)
    by_core(finish_own)

    def step(t, carry):
        left, right = a - t, a + t
        pleft, pright = a - t + 1, a + t - 1
        for u in range(2):
            @pl.when(left >= 0)
            def _():
                s = 2 * left + b
                arrived(s, u)

                @pl.when(a < A - 1)
                def _():
                    push(gath.at[s, u], 0, s, u, me + 2).start()

                @pl.when((left > 0) | (u == 0))
                def _():
                    push(gath.at[s, u], 2, s, u, pair).start()

            @pl.when(right < A)
            def _():
                s = 2 * right + b
                arrived(s, u)

                @pl.when(a > 0)
                def _():
                    push(gath.at[s, u], 1, s, u, me - 2).start()

                @pl.when((right < A - 1) | (u == 0))
                def _():
                    push(gath.at[s, u], 2, s, u, pair).start()

        @pl.when(left == -1)
        def _():
            s = 1 - b
            arrived(s, 1)

            @pl.when(a < A - 1)
            def _():
                push(gath.at[s, 1], 0, s, 1, me + 2).start()

        @pl.when(right == A)
        def _():
            s = 2 * (A - 1) + 1 - b
            arrived(s, 1)

            @pl.when(a > 0)
            def _():
                push(gath.at[s, 1], 1, s, 1, me - 2).start()
        work = (
            (left >= 0, left, b, False),
            (right < A, right, b, False),
            (pleft >= 0, pleft, 1 - b, True),
            ((pright < A) & (t > 1), pright, 1 - b, True),
        )
        for valid, place, column, wait in work:
            s = 2 * place + column

            @pl.when(valid)
            def _():
                if wait:
                    arrived(s, 0)

                    @pl.when((place > 0) & (place < A - 1))
                    def _():
                        arrived(s, 1)
                multiply(s, gath.at[s, 0], gath.at[s, 1])
        for valid, place, column, wait in work:
            s = 2 * place + column

            @pl.when(valid)
            def _():
                finish(s)
        return carry

    lax.fori_loop(1, A + 1, step, 0)

    def place(s, carry):
        at = pl.ds(pl.multiple_of(s * cols, cols), cols)

        def wait(mine, theirs):
            @pl.when(s != me)
            def _():
                home(s, s, s, *mine).wait_recv()
        by_core(wait)

        @pl.when(c == 0)
        def _():
            out[0, :, at] = back[s, :low // 2]
            out[1, :, at] = back[s, low // 2:low]

        @pl.when(c == 1)
        def _():
            both = dot(unpack[...], back[s, low:]).astype(bf16)
            out[0, :, at] = both[:low // 2]
            out[1, :, at] = both[low // 2:]
        return carry

    lax.fori_loop(0, R, place, 0)

    def drain(s, carry):
        sa = s // 2
        mine_col = s - 2 * sa == b

        def fn(mine, theirs):
            exchange(s, *theirs).wait_send()

            @pl.when(s != me)
            def _():
                home(s, me, s, *mine).wait_send()
        by_core(fn)
        for u in range(2):
            @pl.when(mine_col & (sa <= a) & (a < A - 1))
            def _():
                push(packed.at[u], 0, s, u, me + 2).wait_send()

            @pl.when(mine_col & (sa >= a) & (a > 0))
            def _():
                push(packed.at[u], 1, s, u, me - 2).wait_send()

            direct = (sa == a) | (u == 0) | ((sa > 0) & (sa < A - 1))

            @pl.when(mine_col & direct)
            def _():
                push(packed.at[u], 2, s, u, pair).wait_send()

        @pl.when((s == 1 - b) & (a < A - 1))
        def _():
            push(packed.at[1], 0, s, 1, me + 2).wait_send()

        @pl.when((s == 2 * (A - 1) + 1 - b) & (a > 0))
        def _():
            push(packed.at[1], 1, s, 1, me - 2).wait_send()
        return carry

    lax.fori_loop(0, R, drain, 0)


def local(
    value_stream, gate_stream, key_query_stream, step_stream, parents, tree_sizes, slot_index,
    value_cache, key_query_cache, value_conv, key_query_conv, step_bias, log_rate, skip_gain,
    norm_gain, cached_state, out_weight,
):
    Q, N, C = value_stream.shape
    G = key_query_stream.shape[2]
    heads, PD, S = cached_state.shape[1:]
    H = heads // G
    CG = C // G
    R = lax.axis_size("req")
    packed_rows = N + N // 2
    caches = value_cache.transpose(1, 0, 2)
    smem = pl.BlockSpec(memory_space=pltpu.SMEM)
    whole = lambda x: pl.BlockSpec(x.shape, lambda g, r: (0,) * x.ndim)
    by_group = lambda x, n: pl.BlockSpec(x.shape[:-1] + (n,), lambda g, r: (0,) * (x.ndim - 1) + (g,))
    bias, rate, skip = (x.reshape(1, -1) for x in (step_bias, log_rate, skip_gain))
    state_spec = pl.BlockSpec((1, H, PD, S), lambda g, r: (r, g, 0, 0))
    packed, unpack, final_state = pl.pallas_call(
        ssm_kernel,
        grid=(G, Q),
        out_shape=(
            jax.ShapeDtypeStruct((G, packed_rows, CG), bf16),
            jax.ShapeDtypeStruct((N, N // 2), bf16),
            jax.ShapeDtypeStruct(cached_state.shape, f32),
        ),
        in_specs=[
            smem, smem, smem,
            by_group(value_stream, CG), by_group(gate_stream, CG), whole(key_query_stream), whole(step_stream),
            by_group(caches, CG), whole(key_query_cache), by_group(value_conv, CG),
            whole(key_query_conv), whole(bias), whole(rate), whole(skip), pl.BlockSpec((CG,), lambda g, r: (g,)), state_spec,
        ],
        out_specs=(
            pl.BlockSpec((1, packed_rows, CG), lambda g, r: (g, 0, 0)),
            pl.BlockSpec((N, N // 2), lambda g, r: (0, 0)),
            state_spec,
        ),
        scratch_shapes=[
            pltpu.VMEM((2, 3 * N, N), bf16),
            pltpu.VMEM((2 * N, 4 * N), f32),
            pltpu.VMEM((2 * N, 128), f32),
            pltpu.VMEM((2 * N, H), f32),
            pltpu.VMEM((2, 2 * N, H), f32),
            pltpu.VMEM((2, 2 * N, H), f32),
            pltpu.VMEM((2, 8, H), f32),
            pltpu.VMEM((H, CG), bf16),
            pltpu.VMEM((H, H * N), bf16),
        ],
        compiler_params=pltpu.CompilerParams(vmem_limit_bytes=60 * 2**20),
        name="ssm",
    )(
        slot_index, tree_sizes, parents, value_stream, gate_stream, key_query_stream, step_stream, caches,
        key_query_cache, value_conv, key_query_conv, bias, rate, skip, norm_gain, cached_state,
    )
    cols = out_weight.shape[1]
    vmem = pl.BlockSpec(memory_space=pltpu.VMEM)
    dma = pltpu.SemaphoreType.DMA
    out = pl.pallas_call(
        functools.partial(comm_kernel, R),
        out_shape=jax.ShapeDtypeStruct((Q, N // 2, R * cols), bf16),
        in_specs=[vmem, vmem, pl.BlockSpec(memory_space=pl.ANY)],
        out_specs=vmem,
        scratch_shapes=[
            pltpu.VMEM(out_weight.shape, bf16),
            pltpu.VMEM((R, G, packed_rows, CG), bf16),
            pltpu.VMEM((R, packed_rows, cols), f32),
            pltpu.VMEM((R, packed_rows, cols), f32),
            pltpu.VMEM((R, packed_rows, cols), bf16),
            pltpu.VMEM((R, packed_rows, cols), bf16),
            dma, dma((3, R, G)), dma((R, G)), dma((R,)), dma((R,)), dma((R,)), dma((R,)),
        ],
        compiler_params=pltpu.CompilerParams(
            collective_id=0, has_side_effects=True, vmem_limit_bytes=60 * 2**20
        ),
        name="project",
    )(packed, unpack, out_weight)
    return (out, final_state)


def solution(mesh):
    return jax.shard_map(
        local,
        mesh=mesh,
        in_specs=(
            P(("group", "req"), None, "chan"),
            P(("group", "req"), None, "chan"),
            P(("group", "req"), None, "chan", None),
            P(("group", "req"), None, "chan"),
            P(("group", "req"), None),
            P(("group", "req")),
            P(("group", "req")),
            P(("group", "req"), None, "chan"),
            P(("group", "req"), None, "chan", None),
            P(None, "chan"),
            P(None, "chan", None),
            P("chan"),
            P("chan"),
            P("chan"),
            P("chan"),
            P(("group", "req"), "chan", None, None),
            P("chan", "req"),
        ),
        out_specs=(P(("group", "req"), "chan", None), P(("group", "req"), "chan", None, None)),
        check_vma=False,
    )
```

```python
import functools

import jax
import jax.numpy as jnp
from jax import lax
from jax.experimental import pallas as pl
from jax.experimental.pallas import tpu as pltpu
from jax.sharding import PartitionSpec as P

f32 = jnp.float32
bf16 = jnp.bfloat16
highest = lax.Precision.HIGHEST
norm_epsilon = 1e-05
MESH = pl.DeviceIdType.MESH
NT = (((1,), (1,)), ((), ()))
TN = (((0,), (0,)), ((), ()))


def iota(shape, dim):
    return lax.broadcasted_iota(jnp.int32, shape, dim)


def dot(a, b):
    return jnp.dot(a, b, preferred_element_type=f32)


def silu(x):
    return x / (1.0 + jnp.exp(-x))


def spread(x, onehot, terms):
    total = None
    for _ in range(terms):
        part = x.astype(bf16)
        x = x - part.astype(f32)
        term = dot(part, onehot)
        total = term if total is None else total + term
    return total


def ssm_kernel(
    slot_s, size_s, parent_s,
    val_ref, gate_ref, kq_ref, step_ref, vcache_ref, kqcache_ref, vw_ref, kqw_ref,
    bias_ref, rate_ref, skip_ref, gain_ref, state_ref,
    hid_ref, unpack_ref, final_ref,
    shift_sc, anc_sc, depth_sc, last_sc, level_sc, size_sc, skip_sc, chan_sc, lane_sc,
):
    g = pl.program_id(0)
    N = gate_ref.shape[1]
    H = skip_sc.shape[2]
    C = gate_ref.shape[2]
    PD = C // H
    half = N // 2
    slots = [lax.rem(slot_s[k], gate_ref.shape[0]) for k in range(2)]

    @pl.when(g == 0)
    def _():
        M = 2 * N
        rows, cols = iota((M, M), 0), iota((M, M), 1)
        par = jnp.full((M, M), -1, jnp.int32)
        for k in range(2):
            for n in range(1, N):
                par = jnp.where(rows == k * N + n, parent_s[k, n] + k * N, par)
        one = jnp.where(par == cols, 1.0, 0.0).astype(f32)
        eye = jnp.where(rows == cols, 1.0, 0.0).astype(f32)
        step_b = one.astype(bf16)
        second = dot(step_b, step_b)
        third = dot(second.astype(bf16), step_b)
        anc = eye + one
        power = second
        reach = 2
        while reach < N:
            anc = dot(anc.astype(bf16), (eye + power).astype(bf16))
            reach *= 2
            if reach < N:
                power = dot(power.astype(bf16), power.astype(bf16))
        for k in range(2):
            lo, hi = k * N, (k + 1) * N
            for i, mat in enumerate((one, second, third)):
                tile = jnp.where(
                    iota((M, N), 0) - iota((M, N), 1) == lo, 1.0, 0.0
                ).astype(bf16)
                shift_sc[k, i * N:(i + 1) * N, :] = dot(mat[lo:hi].astype(bf16), tile).astype(bf16)
        fold = jnp.where(lax.rem(iota((M, 4 * N), 0), N) == lax.rem(iota((M, 4 * N), 1), N), 1.0, 0.0)
        anc_sc[...] = dot(anc.astype(bf16), fold.astype(bf16))
        depth_sc[...] = jnp.broadcast_to(jnp.sum(anc, axis=1, keepdims=True) - 1.0, depth_sc.shape)
        row_h = iota((M, H), 0)
        pick = (row_h == size_s[0] - 1) | (row_h == N + size_s[1] - 1)
        last_sc[...] = lax.dot_general(
            anc.astype(bf16), jnp.where(pick, 1.0, 0.0).astype(bf16), TN, preferred_element_type=f32
        )
        x = jnp.concatenate([step_ref[slots[0]], step_ref[slots[1]]], axis=0).astype(f32) + bias_ref[...]
        step = jnp.maximum(x, 0.0) + jnp.log1p(jnp.exp(-jnp.abs(x)))
        rate = -jnp.exp(rate_ref[...])
        level = jnp.dot(anc, step * rate, precision=highest, preferred_element_type=f32)
        for k in range(2):
            level_sc[k] = level[:, k * H:(k + 1) * H]
            size_sc[k] = step[:, k * H:(k + 1) * H]
            skip_sc[k] = jnp.broadcast_to(skip_ref[:, k * H:(k + 1) * H], skip_sc.shape[1:])
        chan_sc[...] = jnp.where(iota((H, C), 1) // PD == iota((H, C), 0), 1.0, 0.0).astype(bf16)
        lane_sc[...] = jnp.where(iota((H, H * N), 1) // N == iota((H, H * N), 0), 1.0, 0.0).astype(bf16)
        u_row, u_col = iota((N, half), 0), iota((N, half), 1)
        req = u_row // half
        node = u_row - req * half
        over = jnp.maximum(size_s[0] - half, 0)
        place = node + jnp.where(req == 1, over, 0)
        live = node + half < jnp.where(req == 1, size_s[1], size_s[0])
        unpack_ref[...] = jnp.where((u_col == place) & live, 1.0, 0.0).astype(bf16)

    def row_of(pair, index):
        pair = pair.astype(f32)
        return jnp.where(index == 0, pair[0:1], pair[1:2])

    def conv(x, cache, w, shifts, depth):
        back = dot(shifts, x)
        c0, c1, c2 = cache
        w0, w1, w2, w3 = w
        total = w3 * x.astype(f32)
        for k in range(1, 4):
            total = total + w[3 - k] * back[(k - 1) * N:k * N]
        total = total + jnp.where(depth == 0.0, w2 * c2 + w1 * c1 + w0 * c0, 0.0)
        total = total + jnp.where(depth == 1.0, w1 * c2 + w0 * c1, 0.0)
        total = total + jnp.where(depth == 2.0, w0 * c2, 0.0)
        return silu(total)

    both = range(2)
    S = kq_ref.shape[3] // 2
    own = [slice(r * N, (r + 1) * N) for r in both]
    shifts = [shift_sc[r] for r in both]
    depth = [depth_sc[own[r], 0:1] for r in both]
    kq_taps = [row_of(kqw_ref[k], g) for k in range(4)]
    kq = []
    for r in both:
        rows = jnp.where(
            g == 0, kq_ref[slots[r], :, 0, :].astype(f32), kq_ref[slots[r], :, 1, :].astype(f32)
        )
        cache = [row_of(kqcache_ref[r, k], g) for k in range(3)]
        kq.append(conv(rows.astype(bf16), cache, kq_taps, shifts[r], depth[r]))
    key_b = [x[:, :S].astype(bf16) for x in kq]
    query_b = [x[:, S:].astype(bf16) for x in kq]
    levels = level_sc[g]
    steps = size_sc[g]
    stack, decay_m = [], []
    for r in both:
        level = levels[own[r]]
        level_m = jnp.sum(
            jnp.where(iota((N, H), 0) == size_s[r] - 1, level, 0.0), axis=0, keepdims=True
        )
        last_decay = jnp.exp(jnp.where(last_sc[own[r], :] > 0.5, level_m - level, -1e30))
        decay_m.append(jnp.exp(level_m))
        stack += [steps[own[r]], jnp.exp(level), last_decay]
    wide = spread(jnp.concatenate(stack + [skip_sc[g]], axis=0), chan_sc[...], 2)
    level_all = spread(levels, lane_sc[...], 3)
    diag = lax.rem(iota((N, H * N), 1), N) == iota((N, H * N), 0)
    level_x = [level_all[own[r]] for r in both]
    level_row = [jnp.sum(jnp.where(diag, x, 0.0), axis=0, keepdims=True) for x in level_x]
    anc4 = [anc_sc[own[r], :] > 0.5 for r in both]
    affinity4 = [
        lax.dot_general(
            x[:, S:], jnp.concatenate([x[:, :S]] * 4, axis=0), NT, precision=highest,
            preferred_element_type=f32,
        )
        for x in kq
    ]
    block_mask = iota((4 * N, 4 * PD), 0) // N == iota((4 * N, 4 * PD), 1) // PD

    pieces = [[], []]
    for q in range(H // 4):
        cs = slice(q * 4 * PD, (q + 1) * 4 * PD)
        ls = slice(q * 4 * N, (q + 1) * 4 * N)
        taps = vw_ref[:, cs].astype(f32)
        taps = [taps[k:k + 1] for k in range(4)]
        skip = wide[6 * N:6 * N + 1, cs]
        for r in both:
            base = 3 * N * r
            cache = [row_of(vcache_ref[k, :, cs], r) for k in range(3)]
            values = conv(val_ref[slots[r], :, cs], cache, taps, shifts[r], depth[r])
            gap = level_x[r][:, ls] - level_row[r][:, ls]
            weights = affinity4[r] * jnp.exp(jnp.where(anc4[r], gap, -1e30))
            stepped = values * wide[base:base + N, cs]
            four = jnp.concatenate([stepped] * 4, axis=0)
            four = jnp.where(block_mask, four, 0.0).astype(bf16)
            inner = dot(weights.astype(bf16), four)
            state = state_ref[r, 4 * q:4 * q + 4].reshape(4 * PD, S)
            carried = lax.dot_general(query_b[r], state.astype(bf16), NT, preferred_element_type=f32)
            result = inner + carried * wide[base + N:base + 2 * N, cs] + skip * values
            pieces[r].append(result * silu(gate_ref[slots[r], :, cs].astype(f32)))
            scaled = (stepped * wide[base + 2 * N:base + 3 * N, cs]).astype(bf16)
            update = lax.dot_general(scaled, key_b[r], TN, preferred_element_type=f32)
            for k in range(4):
                h = 4 * q + k
                final_ref[r, h] = (
                    jnp.broadcast_to(decay_m[r][:, h:h + 1], (PD, S)) * state_ref[r, h]
                    + update[k * PD:(k + 1) * PD]
                )
    inverse, live, pack = [], [], []
    for r in both:
        square = sum(jnp.sum(p * p, axis=1, keepdims=True) for p in pieces[r])
        inverse.append(lax.rsqrt(square / C + norm_epsilon))
        live.append(iota((N, 1), 0) < size_s[r])
        over = jnp.maximum(size_s[0] - half, 0) * r
        pack.append(
            jnp.where(iota((half, half), 0) == iota((half, half), 1) + over, 1.0, 0.0).astype(bf16)
        )
    for q in range(H // 4):
        cs = slice(q * 4 * PD, (q + 1) * 4 * PD)
        gain = gain_ref[cs].astype(f32).reshape(1, -1)
        tail = None
        for r in both:
            hidden = jnp.where(live[r], pieces[r][q] * inverse[r] * gain, 0.0).astype(bf16)
            hid_ref[0, r * half:(r + 1) * half, cs] = hidden[:half]
            term = dot(pack[r], hidden[half:])
            tail = term if tail is None else tail + term
        hid_ref[0, N:, cs] = tail.astype(bf16)


def comm_kernel(
    R, packed, unpack, w_any, out,
    wbuf, gath, part, other, fin, back,
    w_sem, send_sem, recv_sem, ex_send, ex_recv, home_send, home_recv,
):
    gi, me, c = lax.axis_index("group"), lax.axis_index("req"), lax.axis_index("chan")
    A = R // 2
    a = me // 2
    b = me - 2 * a
    pair = 2 * a + 1 - b
    cols = wbuf.shape[1]
    rows = gath.shape[2]
    low = out.shape[1] * 2
    wcopy = pltpu.make_async_copy(w_any, wbuf, w_sem)
    wcopy.start()

    barrier = pltpu.get_barrier_semaphore()
    for k in range(1, R):
        pl.semaphore_signal(barrier, inc=1, device_id=(gi, lax.rem(me + k, R), c), device_id_type=MESH)
    pl.semaphore_signal(barrier, inc=1, device_id=(gi, me, 1 - c), device_id_type=MESH)
    pl.semaphore_wait(barrier, R)

    def push(src, way, slot, u, target):
        return pltpu.make_async_remote_copy(
            src_ref=src, dst_ref=gath.at[slot, u],
            send_sem=send_sem.at[way, slot, u], recv_sem=recv_sem.at[slot, u],
            device_id=(gi, target, c), device_id_type=MESH,
        )

    def arrived(slot, u):
        push(gath.at[slot, u], 0, slot, u, pair).wait_recv()

    def exchange(slot, lo, hi):
        return pltpu.make_async_remote_copy(
            src_ref=part.at[slot, lo:hi], dst_ref=other.at[slot, lo:hi],
            send_sem=ex_send.at[slot], recv_sem=ex_recv.at[slot],
            device_id=(gi, me, 1 - c), device_id_type=MESH,
        )

    def home(slot, place, target, lo, hi):
        return pltpu.make_async_remote_copy(
            src_ref=fin.at[slot, lo:hi], dst_ref=back.at[place, lo:hi],
            send_sem=home_send.at[slot], recv_sem=home_recv.at[place],
            device_id=(gi, target, c), device_id_type=MESH,
        )

    def by_core(fn):
        @pl.when(c == 0)
        def _():
            fn((0, low), (low, rows))

        @pl.when(c == 1)
        def _():
            fn((low, rows), (0, low))

    depth = gath.shape[3]

    def multiply(slot, first, second):
        @pl.loop(0, cols // 256)
        def _(t):
            at = pl.ds(pl.multiple_of(t * 256, 256), 256)
            part[slot, :, at] = dot(first[...], wbuf[:depth, at]) + dot(second[...], wbuf[depth:, at])
        by_core(lambda mine, theirs: exchange(slot, *theirs).start())

    def finish(slot):
        def fn(mine, theirs):
            exchange(slot, *mine).wait_recv()
            at = slice(*mine)
            fin[slot, at] = (part[slot, at] + other[slot, at]).astype(bf16)
            home(slot, me, slot, *mine).start()
        by_core(fn)

    for u in range(2):
        @pl.when(a < A - 1)
        def _():
            push(packed.at[u], 0, me, u, me + 2).start()

        @pl.when(a > 0)
        def _():
            push(packed.at[u], 1, me, u, me - 2).start()
        push(packed.at[u], 2, me, u, pair).start()

    wcopy.wait()
    multiply(me, packed.at[0], packed.at[1])

    def finish_own(mine, theirs):
        exchange(me, *mine).wait_recv()
        at = slice(*mine)
        back[me, at] = (part[me, at] + other[me, at]).astype(bf16)
    by_core(finish_own)

    def step(t, carry):
        left, right = a - t, a + t
        pleft, pright = a - t + 1, a + t - 1
        for u in range(2):
            @pl.when(left >= 0)
            def _():
                s = 2 * left + b
                arrived(s, u)

                @pl.when(a < A - 1)
                def _():
                    push(gath.at[s, u], 0, s, u, me + 2).start()

                @pl.when((left > 0) | (u == 0))
                def _():
                    push(gath.at[s, u], 2, s, u, pair).start()

            @pl.when(right < A)
            def _():
                s = 2 * right + b
                arrived(s, u)

                @pl.when(a > 0)
                def _():
                    push(gath.at[s, u], 1, s, u, me - 2).start()

                @pl.when((right < A - 1) | (u == 0))
                def _():
                    push(gath.at[s, u], 2, s, u, pair).start()

        @pl.when(left == -1)
        def _():
            s = 1 - b
            arrived(s, 1)

            @pl.when(a < A - 1)
            def _():
                push(gath.at[s, 1], 0, s, 1, me + 2).start()

        @pl.when(right == A)
        def _():
            s = 2 * (A - 1) + 1 - b
            arrived(s, 1)

            @pl.when(a > 0)
            def _():
                push(gath.at[s, 1], 1, s, 1, me - 2).start()
        work = (
            (left >= 0, left, b, False),
            (right < A, right, b, False),
            (pleft >= 0, pleft, 1 - b, True),
            ((pright < A) & (t > 1), pright, 1 - b, True),
        )
        for valid, place, column, wait in work:
            s = 2 * place + column

            @pl.when(valid)
            def _():
                if wait:
                    arrived(s, 0)

                    @pl.when((place > 0) & (place < A - 1))
                    def _():
                        arrived(s, 1)
                multiply(s, gath.at[s, 0], gath.at[s, 1])
        for valid, place, column, wait in work:
            s = 2 * place + column

            @pl.when(valid)
            def _():
                finish(s)
        return carry

    lax.fori_loop(1, A + 1, step, 0)

    def place(s, carry):
        at = pl.ds(pl.multiple_of(s * cols, cols), cols)

        def wait(mine, theirs):
            @pl.when(s != me)
            def _():
                home(s, s, s, *mine).wait_recv()
        by_core(wait)

        @pl.when(c == 0)
        def _():
            out[0, :, at] = back[s, :low // 2]
            out[1, :, at] = back[s, low // 2:low]

        @pl.when(c == 1)
        def _():
            both = dot(unpack[...], back[s, low:]).astype(bf16)
            out[0, :, at] = both[:low // 2]
            out[1, :, at] = both[low // 2:]
        return carry

    lax.fori_loop(0, R, place, 0)

    def drain(s, carry):
        sa = s // 2
        mine_col = s - 2 * sa == b

        def fn(mine, theirs):
            exchange(s, *theirs).wait_send()

            @pl.when(s != me)
            def _():
                home(s, me, s, *mine).wait_send()
        by_core(fn)
        for u in range(2):
            @pl.when(mine_col & (sa <= a) & (a < A - 1))
            def _():
                push(packed.at[u], 0, s, u, me + 2).wait_send()

            @pl.when(mine_col & (sa >= a) & (a > 0))
            def _():
                push(packed.at[u], 1, s, u, me - 2).wait_send()

            direct = (sa == a) | (u == 0) | ((sa > 0) & (sa < A - 1))

            @pl.when(mine_col & direct)
            def _():
                push(packed.at[u], 2, s, u, pair).wait_send()

        @pl.when((s == 1 - b) & (a < A - 1))
        def _():
            push(packed.at[1], 0, s, 1, me + 2).wait_send()

        @pl.when((s == 2 * (A - 1) + 1 - b) & (a > 0))
        def _():
            push(packed.at[1], 1, s, 1, me - 2).wait_send()
        return carry

    lax.fori_loop(0, R, drain, 0)


def local(
    value_stream, gate_stream, key_query_stream, step_stream, parents, tree_sizes, slot_index,
    value_cache, key_query_cache, value_conv, key_query_conv, step_bias, log_rate, skip_gain,
    norm_gain, cached_state, out_weight,
):
    Q, N, C = value_stream.shape
    G = key_query_stream.shape[2]
    heads, PD, S = cached_state.shape[1:]
    H = heads // G
    CG = C // G
    R = lax.axis_size("req")
    packed_rows = N + N // 2
    caches = value_cache.transpose(1, 0, 2)
    smem = pl.BlockSpec(memory_space=pltpu.SMEM)
    whole = lambda x: pl.BlockSpec(x.shape, lambda g: (0,) * x.ndim)
    by_group = lambda x, n: pl.BlockSpec(x.shape[:-1] + (n,), lambda g: (0,) * (x.ndim - 1) + (g,))
    bias, rate, skip = (x.reshape(1, -1) for x in (step_bias, log_rate, skip_gain))
    state_spec = pl.BlockSpec((Q, H, PD, S), lambda g: (0, g, 0, 0))
    packed, unpack, final_state = pl.pallas_call(
        ssm_kernel,
        grid=(G,),
        out_shape=(
            jax.ShapeDtypeStruct((G, packed_rows, CG), bf16),
            jax.ShapeDtypeStruct((N, N // 2), bf16),
            jax.ShapeDtypeStruct(cached_state.shape, f32),
        ),
        in_specs=[
            smem, smem, smem,
            by_group(value_stream, CG), by_group(gate_stream, CG), whole(key_query_stream), whole(step_stream),
            by_group(caches, CG), whole(key_query_cache), by_group(value_conv, CG),
            whole(key_query_conv), whole(bias), whole(rate), whole(skip), pl.BlockSpec((CG,), lambda g: (g,)), state_spec,
        ],
        out_specs=(
            pl.BlockSpec((1, packed_rows, CG), lambda g: (g, 0, 0)),
            pl.BlockSpec((N, N // 2), lambda g: (0, 0)),
            state_spec,
        ),
        scratch_shapes=[
            pltpu.VMEM((2, 3 * N, N), bf16),
            pltpu.VMEM((2 * N, 4 * N), f32),
            pltpu.VMEM((2 * N, 128), f32),
            pltpu.VMEM((2 * N, H), f32),
            pltpu.VMEM((2, 2 * N, H), f32),
            pltpu.VMEM((2, 2 * N, H), f32),
            pltpu.VMEM((2, 8, H), f32),
            pltpu.VMEM((H, CG), bf16),
            pltpu.VMEM((H, H * N), bf16),
        ],
        compiler_params=pltpu.CompilerParams(vmem_limit_bytes=60 * 2**20),
        name="ssm",
    )(
        slot_index, tree_sizes, parents, value_stream, gate_stream, key_query_stream, step_stream, caches,
        key_query_cache, value_conv, key_query_conv, bias, rate, skip, norm_gain, cached_state,
    )
    cols = out_weight.shape[1]
    vmem = pl.BlockSpec(memory_space=pltpu.VMEM)
    dma = pltpu.SemaphoreType.DMA
    out = pl.pallas_call(
        functools.partial(comm_kernel, R),
        out_shape=jax.ShapeDtypeStruct((Q, N // 2, R * cols), bf16),
        in_specs=[vmem, vmem, pl.BlockSpec(memory_space=pl.ANY)],
        out_specs=vmem,
        scratch_shapes=[
            pltpu.VMEM(out_weight.shape, bf16),
            pltpu.VMEM((R, G, packed_rows, CG), bf16),
            pltpu.VMEM((R, packed_rows, cols), f32),
            pltpu.VMEM((R, packed_rows, cols), f32),
            pltpu.VMEM((R, packed_rows, cols), bf16),
            pltpu.VMEM((R, packed_rows, cols), bf16),
            dma, dma((3, R, G)), dma((R, G)), dma((R,)), dma((R,)), dma((R,)), dma((R,)),
        ],
        compiler_params=pltpu.CompilerParams(
            collective_id=0, has_side_effects=True, vmem_limit_bytes=60 * 2**20
        ),
        name="project",
    )(packed, unpack, out_weight)
    return (out, final_state)


def solution(mesh):
    return jax.shard_map(
        local,
        mesh=mesh,
        in_specs=(
            P(("group", "req"), None, "chan"),
            P(("group", "req"), None, "chan"),
            P(("group", "req"), None, "chan", None),
            P(("group", "req"), None, "chan"),
            P(("group", "req"), None),
            P(("group", "req")),
            P(("group", "req")),
            P(("group", "req"), None, "chan"),
            P(("group", "req"), None, "chan", None),
            P(None, "chan"),
            P(None, "chan", None),
            P("chan"),
            P("chan"),
            P("chan"),
            P("chan"),
            P(("group", "req"), "chan", None, None),
            P("chan", "req"),
        ),
        out_specs=(P(("group", "req"), "chan", None), P(("group", "req"), "chan", None, None)),
        check_vma=False,
    )
```

```python
import functools

import jax
import jax.numpy as jnp
from jax import lax
from jax.experimental import pallas as pl
from jax.experimental.pallas import tpu as pltpu
from jax.sharding import PartitionSpec as P

f32 = jnp.float32
bf16 = jnp.bfloat16
highest = lax.Precision.HIGHEST
norm_epsilon = 1e-05
MESH = pl.DeviceIdType.MESH
NT = (((1,), (1,)), ((), ()))
TN = (((0,), (0,)), ((), ()))


def iota(shape, dim):
    return lax.broadcasted_iota(jnp.int32, shape, dim)


def dot(a, b):
    return jnp.dot(a, b, preferred_element_type=f32)


def silu(x):
    return x / (1.0 + jnp.exp(-x))


def spread(x, onehot, terms):
    total = None
    for _ in range(terms):
        part = x.astype(bf16)
        x = x - part.astype(f32)
        term = dot(part, onehot)
        total = term if total is None else total + term
    return total


def ssm_kernel(
    slot_s, size_s, parent_s,
    val_ref, gate_ref, kq_ref, step_ref, vcache_ref, kqcache_ref, vw_ref, kqw_ref,
    bias_ref, rate_ref, skip_ref, gain_ref, state_ref,
    hid_ref, unpack_ref, final_ref,
    shift_sc, anc_sc, depth_sc, last_sc, level_sc, size_sc, skip_sc, chan_sc, lane_sc,
):
    g = pl.program_id(0)
    N = gate_ref.shape[1]
    H = skip_sc.shape[2]
    C = gate_ref.shape[2]
    PD = C // H
    half = N // 2
    slots = [lax.rem(slot_s[k], gate_ref.shape[0]) for k in range(2)]

    @pl.when(g == 0)
    def _():
        M = 2 * N
        rows, cols = iota((M, M), 0), iota((M, M), 1)
        par = jnp.full((M, M), -1, jnp.int32)
        for k in range(2):
            for n in range(1, N):
                par = jnp.where(rows == k * N + n, parent_s[k, n] + k * N, par)
        one = jnp.where(par == cols, 1.0, 0.0).astype(f32)
        eye = jnp.where(rows == cols, 1.0, 0.0).astype(f32)
        step_b = one.astype(bf16)
        second = dot(step_b, step_b)
        third = dot(second.astype(bf16), step_b)
        anc = eye + one
        power = second
        reach = 2
        while reach < N:
            anc = dot(anc.astype(bf16), (eye + power).astype(bf16))
            reach *= 2
            if reach < N:
                power = dot(power.astype(bf16), power.astype(bf16))
        for k in range(2):
            lo, hi = k * N, (k + 1) * N
            for i, mat in enumerate((one, second, third)):
                tile = jnp.where(
                    iota((M, N), 0) - iota((M, N), 1) == lo, 1.0, 0.0
                ).astype(bf16)
                shift_sc[k, i * N:(i + 1) * N, :] = dot(mat[lo:hi].astype(bf16), tile).astype(bf16)
        fold = jnp.where(lax.rem(iota((M, 4 * N), 0), N) == lax.rem(iota((M, 4 * N), 1), N), 1.0, 0.0)
        anc_sc[...] = dot(anc.astype(bf16), fold.astype(bf16))
        depth_sc[...] = jnp.broadcast_to(jnp.sum(anc, axis=1, keepdims=True) - 1.0, depth_sc.shape)
        row_h = iota((M, H), 0)
        pick = (row_h == size_s[0] - 1) | (row_h == N + size_s[1] - 1)
        last_sc[...] = lax.dot_general(
            anc.astype(bf16), jnp.where(pick, 1.0, 0.0).astype(bf16), TN, preferred_element_type=f32
        )
        x = jnp.concatenate([step_ref[slots[0]], step_ref[slots[1]]], axis=0).astype(f32) + bias_ref[...]
        step = jnp.maximum(x, 0.0) + jnp.log1p(jnp.exp(-jnp.abs(x)))
        rate = -jnp.exp(rate_ref[...])
        level = jnp.dot(anc, step * rate, precision=highest, preferred_element_type=f32)
        for k in range(2):
            level_sc[k] = level[:, k * H:(k + 1) * H]
            size_sc[k] = step[:, k * H:(k + 1) * H]
            skip_sc[k] = jnp.broadcast_to(skip_ref[:, k * H:(k + 1) * H], skip_sc.shape[1:])
        chan_sc[...] = jnp.where(iota((H, C), 1) // PD == iota((H, C), 0), 1.0, 0.0).astype(bf16)
        lane_sc[...] = jnp.where(iota((H, H * N), 1) // N == iota((H, H * N), 0), 1.0, 0.0).astype(bf16)
        u_row, u_col = iota((N, half), 0), iota((N, half), 1)
        req = u_row // half
        node = u_row - req * half
        over = jnp.maximum(size_s[0] - half, 0)
        place = node + jnp.where(req == 1, over, 0)
        live = node + half < jnp.where(req == 1, size_s[1], size_s[0])
        unpack_ref[...] = jnp.where((u_col == place) & live, 1.0, 0.0).astype(bf16)

    def row_of(pair, index):
        pair = pair.astype(f32)
        return jnp.where(index == 0, pair[0:1], pair[1:2])

    def conv(x, cache, w, shifts, depth):
        back = dot(shifts, x)
        c0, c1, c2 = cache
        w0, w1, w2, w3 = w
        total = w3 * x.astype(f32)
        for k in range(1, 4):
            total = total + w[3 - k] * back[(k - 1) * N:k * N]
        total = total + jnp.where(depth == 0.0, w2 * c2 + w1 * c1 + w0 * c0, 0.0)
        total = total + jnp.where(depth == 1.0, w1 * c2 + w0 * c1, 0.0)
        total = total + jnp.where(depth == 2.0, w0 * c2, 0.0)
        return silu(total)

    both = range(2)
    S = kq_ref.shape[3] // 2
    own = [slice(r * N, (r + 1) * N) for r in both]
    shifts = [shift_sc[r] for r in both]
    depth = [depth_sc[own[r], 0:1] for r in both]
    kq_taps = [row_of(kqw_ref[k], g) for k in range(4)]
    kq = []
    for r in both:
        rows = jnp.where(
            g == 0, kq_ref[slots[r], :, 0, :].astype(f32), kq_ref[slots[r], :, 1, :].astype(f32)
        )
        cache = [row_of(kqcache_ref[r, k], g) for k in range(3)]
        kq.append(conv(rows.astype(bf16), cache, kq_taps, shifts[r], depth[r]))
    key_b = [x[:, :S].astype(bf16) for x in kq]
    query_b = [x[:, S:].astype(bf16) for x in kq]
    levels = level_sc[g]
    steps = size_sc[g]
    stack, decay_m = [], []
    for r in both:
        level = levels[own[r]]
        level_m = jnp.sum(
            jnp.where(iota((N, H), 0) == size_s[r] - 1, level, 0.0), axis=0, keepdims=True
        )
        last_decay = jnp.exp(jnp.where(last_sc[own[r], :] > 0.5, level_m - level, -1e30))
        decay_m.append(jnp.exp(level_m))
        stack += [steps[own[r]], jnp.exp(level), last_decay]
    wide = spread(jnp.concatenate(stack + [skip_sc[g]], axis=0), chan_sc[...], 2)
    level_all = spread(levels, lane_sc[...], 3)
    diag = lax.rem(iota((N, H * N), 1), N) == iota((N, H * N), 0)
    level_x = [level_all[own[r]] for r in both]
    level_row = [jnp.sum(jnp.where(diag, x, 0.0), axis=0, keepdims=True) for x in level_x]
    anc4 = [anc_sc[own[r], :] > 0.5 for r in both]
    affinity4 = [
        lax.dot_general(
            x[:, S:], jnp.concatenate([x[:, :S]] * 4, axis=0), NT, precision=highest,
            preferred_element_type=f32,
        )
        for x in kq
    ]
    block_mask = iota((4 * N, 4 * PD), 0) // N == iota((4 * N, 4 * PD), 1) // PD

    pieces = [[], []]
    for q in range(H // 4):
        cs = slice(q * 4 * PD, (q + 1) * 4 * PD)
        ls = slice(q * 4 * N, (q + 1) * 4 * N)
        taps = vw_ref[:, cs].astype(f32)
        taps = [taps[k:k + 1] for k in range(4)]
        skip = wide[6 * N:6 * N + 1, cs]
        for r in both:
            base = 3 * N * r
            cache = [row_of(vcache_ref[k, :, cs], r) for k in range(3)]
            values = conv(val_ref[slots[r], :, cs], cache, taps, shifts[r], depth[r])
            gap = level_x[r][:, ls] - level_row[r][:, ls]
            weights = affinity4[r] * jnp.exp(jnp.where(anc4[r], gap, -1e30))
            stepped = values * wide[base:base + N, cs]
            four = jnp.concatenate([stepped] * 4, axis=0)
            four = jnp.where(block_mask, four, 0.0).astype(bf16)
            inner = dot(weights.astype(bf16), four)
            state = state_ref[r, 4 * q:4 * q + 4].reshape(4 * PD, S)
            carried = lax.dot_general(query_b[r], state.astype(bf16), NT, preferred_element_type=f32)
            result = inner + carried * wide[base + N:base + 2 * N, cs] + skip * values
            pieces[r].append(result * silu(gate_ref[slots[r], :, cs].astype(f32)))
            scaled = (stepped * wide[base + 2 * N:base + 3 * N, cs]).astype(bf16)
            update = lax.dot_general(scaled, key_b[r], TN, preferred_element_type=f32)
            for k in range(4):
                h = 4 * q + k
                final_ref[r, h] = (
                    jnp.broadcast_to(decay_m[r][:, h:h + 1], (PD, S)) * state_ref[r, h]
                    + update[k * PD:(k + 1) * PD]
                )
    inverse, live, pack = [], [], []
    for r in both:
        square = sum(jnp.sum(p * p, axis=1, keepdims=True) for p in pieces[r])
        inverse.append(lax.rsqrt(square / C + norm_epsilon))
        live.append(iota((N, 1), 0) < size_s[r])
        over = jnp.maximum(size_s[0] - half, 0) * r
        pack.append(
            jnp.where(iota((half, half), 0) == iota((half, half), 1) + over, 1.0, 0.0).astype(bf16)
        )
    for q in range(H // 4):
        cs = slice(q * 4 * PD, (q + 1) * 4 * PD)
        gain = gain_ref[cs].astype(f32).reshape(1, -1)
        tail = None
        for r in both:
            hidden = jnp.where(live[r], pieces[r][q] * inverse[r] * gain, 0.0).astype(bf16)
            hid_ref[0, r * half:(r + 1) * half, cs] = hidden[:half]
            term = dot(pack[r], hidden[half:])
            tail = term if tail is None else tail + term
        hid_ref[0, N:, cs] = tail.astype(bf16)


def comm_kernel(
    R, packed, unpack, w_any, out,
    wbuf, gath, part, other, fin, back,
    w_sem, send_sem, recv_sem, ex_send, ex_recv, home_send, home_recv,
):
    gi, me, c = lax.axis_index("group"), lax.axis_index("req"), lax.axis_index("chan")
    A = R // 2
    a = me // 2
    b = me - 2 * a
    pair = 2 * a + 1 - b
    cols = wbuf.shape[1]
    rows = gath.shape[2]
    low = out.shape[1] * 2
    wcopy = pltpu.make_async_copy(w_any, wbuf, w_sem)
    wcopy.start()

    barrier = pltpu.get_barrier_semaphore()
    for k in range(1, R):
        pl.semaphore_signal(barrier, inc=1, device_id=(gi, lax.rem(me + k, R), c), device_id_type=MESH)
    pl.semaphore_signal(barrier, inc=1, device_id=(gi, me, 1 - c), device_id_type=MESH)
    pl.semaphore_wait(barrier, R)

    def push(src, way, slot, u, target):
        return pltpu.make_async_remote_copy(
            src_ref=src, dst_ref=gath.at[slot, u],
            send_sem=send_sem.at[way, slot, u], recv_sem=recv_sem.at[slot, u],
            device_id=(gi, target, c), device_id_type=MESH,
        )

    def arrived(slot, u):
        push(gath.at[slot, u], 0, slot, u, pair).wait_recv()

    def exchange(slot, lo, hi):
        return pltpu.make_async_remote_copy(
            src_ref=part.at[slot, lo:hi], dst_ref=other.at[slot, lo:hi],
            send_sem=ex_send.at[slot], recv_sem=ex_recv.at[slot],
            device_id=(gi, me, 1 - c), device_id_type=MESH,
        )

    def home(slot, place, target, lo, hi):
        return pltpu.make_async_remote_copy(
            src_ref=fin.at[slot, lo:hi], dst_ref=back.at[place, lo:hi],
            send_sem=home_send.at[slot], recv_sem=home_recv.at[place],
            device_id=(gi, target, c), device_id_type=MESH,
        )

    def by_core(fn):
        @pl.when(c == 0)
        def _():
            fn((0, low), (low, rows))

        @pl.when(c == 1)
        def _():
            fn((low, rows), (0, low))

    depth = gath.shape[3]

    def multiply(slot, first, second):
        @pl.loop(0, cols // 512)
        def _(t):
            at = pl.ds(pl.multiple_of(t * 512, 512), 512)
            part[slot, :, at] = dot(first[...], wbuf[:depth, at]) + dot(second[...], wbuf[depth:, at])
        by_core(lambda mine, theirs: exchange(slot, *theirs).start())

    def finish(slot):
        def fn(mine, theirs):
            exchange(slot, *mine).wait_recv()
            at = slice(*mine)
            fin[slot, at] = (part[slot, at] + other[slot, at]).astype(bf16)
            home(slot, me, slot, *mine).start()
        by_core(fn)

    for u in range(2):
        @pl.when(a < A - 1)
        def _():
            push(packed.at[u], 0, me, u, me + 2).start()

        @pl.when(a > 0)
        def _():
            push(packed.at[u], 1, me, u, me - 2).start()
        push(packed.at[u], 2, me, u, pair).start()

    wcopy.wait()
    multiply(me, packed.at[0], packed.at[1])

    def finish_own(mine, theirs):
        exchange(me, *mine).wait_recv()
        at = slice(*mine)
        back[me, at] = (part[me, at] + other[me, at]).astype(bf16)
    by_core(finish_own)

    def step(t, carry):
        left, right = a - t, a + t
        pleft, pright = a - t + 1, a + t - 1
        for u in range(2):
            @pl.when(left >= 0)
            def _():
                s = 2 * left + b
                arrived(s, u)

                @pl.when(a < A - 1)
                def _():
                    push(gath.at[s, u], 0, s, u, me + 2).start()

                @pl.when((left > 0) | (u == 0))
                def _():
                    push(gath.at[s, u], 2, s, u, pair).start()

            @pl.when(right < A)
            def _():
                s = 2 * right + b
                arrived(s, u)

                @pl.when(a > 0)
                def _():
                    push(gath.at[s, u], 1, s, u, me - 2).start()

                @pl.when((right < A - 1) | (u == 0))
                def _():
                    push(gath.at[s, u], 2, s, u, pair).start()

        @pl.when(left == -1)
        def _():
            s = 1 - b
            arrived(s, 1)

            @pl.when(a < A - 1)
            def _():
                push(gath.at[s, 1], 0, s, 1, me + 2).start()

        @pl.when(right == A)
        def _():
            s = 2 * (A - 1) + 1 - b
            arrived(s, 1)

            @pl.when(a > 0)
            def _():
                push(gath.at[s, 1], 1, s, 1, me - 2).start()
        work = (
            (left >= 0, left, b, False),
            (right < A, right, b, False),
            (pleft >= 0, pleft, 1 - b, True),
            ((pright < A) & (t > 1), pright, 1 - b, True),
        )
        for valid, place, column, wait in work:
            s = 2 * place + column

            @pl.when(valid)
            def _():
                if wait:
                    arrived(s, 0)

                    @pl.when((place > 0) & (place < A - 1))
                    def _():
                        arrived(s, 1)
                multiply(s, gath.at[s, 0], gath.at[s, 1])
        for valid, place, column, wait in work:
            s = 2 * place + column

            @pl.when(valid)
            def _():
                finish(s)
        return carry

    lax.fori_loop(1, A + 1, step, 0)

    def place(s, carry):
        at = pl.ds(pl.multiple_of(s * cols, cols), cols)

        def wait(mine, theirs):
            @pl.when(s != me)
            def _():
                home(s, s, s, *mine).wait_recv()
        by_core(wait)

        @pl.when(c == 0)
        def _():
            out[0, :, at] = back[s, :low // 2]
            out[1, :, at] = back[s, low // 2:low]

        @pl.when(c == 1)
        def _():
            both = dot(unpack[...], back[s, low:]).astype(bf16)
            out[0, :, at] = both[:low // 2]
            out[1, :, at] = both[low // 2:]
        return carry

    lax.fori_loop(0, R, place, 0)

    def drain(s, carry):
        sa = s // 2
        mine_col = s - 2 * sa == b

        def fn(mine, theirs):
            exchange(s, *theirs).wait_send()

            @pl.when(s != me)
            def _():
                home(s, me, s, *mine).wait_send()
        by_core(fn)
        for u in range(2):
            @pl.when(mine_col & (sa <= a) & (a < A - 1))
            def _():
                push(packed.at[u], 0, s, u, me + 2).wait_send()

            @pl.when(mine_col & (sa >= a) & (a > 0))
            def _():
                push(packed.at[u], 1, s, u, me - 2).wait_send()

            direct = (sa == a) | (u == 0) | ((sa > 0) & (sa < A - 1))

            @pl.when(mine_col & direct)
            def _():
                push(packed.at[u], 2, s, u, pair).wait_send()

        @pl.when((s == 1 - b) & (a < A - 1))
        def _():
            push(packed.at[1], 0, s, 1, me + 2).wait_send()

        @pl.when((s == 2 * (A - 1) + 1 - b) & (a > 0))
        def _():
            push(packed.at[1], 1, s, 1, me - 2).wait_send()
        return carry

    lax.fori_loop(0, R, drain, 0)


def local(
    value_stream, gate_stream, key_query_stream, step_stream, parents, tree_sizes, slot_index,
    value_cache, key_query_cache, value_conv, key_query_conv, step_bias, log_rate, skip_gain,
    norm_gain, cached_state, out_weight,
):
    Q, N, C = value_stream.shape
    G = key_query_stream.shape[2]
    heads, PD, S = cached_state.shape[1:]
    H = heads // G
    CG = C // G
    R = lax.axis_size("req")
    packed_rows = N + N // 2
    caches = value_cache.transpose(1, 0, 2)
    smem = pl.BlockSpec(memory_space=pltpu.SMEM)
    whole = lambda x: pl.BlockSpec(x.shape, lambda g: (0,) * x.ndim)
    by_group = lambda x, n: pl.BlockSpec(x.shape[:-1] + (n,), lambda g: (0,) * (x.ndim - 1) + (g,))
    bias, rate, skip = (x.reshape(1, -1) for x in (step_bias, log_rate, skip_gain))
    state_spec = pl.BlockSpec((Q, H, PD, S), lambda g: (0, g, 0, 0))
    packed, unpack, final_state = pl.pallas_call(
        ssm_kernel,
        grid=(G,),
        out_shape=(
            jax.ShapeDtypeStruct((G, packed_rows, CG), bf16),
            jax.ShapeDtypeStruct((N, N // 2), bf16),
            jax.ShapeDtypeStruct(cached_state.shape, f32),
        ),
        in_specs=[
            smem, smem, smem,
            by_group(value_stream, CG), by_group(gate_stream, CG), whole(key_query_stream), whole(step_stream),
            by_group(caches, CG), whole(key_query_cache), by_group(value_conv, CG),
            whole(key_query_conv), whole(bias), whole(rate), whole(skip), pl.BlockSpec((CG,), lambda g: (g,)), state_spec,
        ],
        out_specs=(
            pl.BlockSpec((1, packed_rows, CG), lambda g: (g, 0, 0)),
            pl.BlockSpec((N, N // 2), lambda g: (0, 0)),
            state_spec,
        ),
        scratch_shapes=[
            pltpu.VMEM((2, 3 * N, N), bf16),
            pltpu.VMEM((2 * N, 4 * N), f32),
            pltpu.VMEM((2 * N, 128), f32),
            pltpu.VMEM((2 * N, H), f32),
            pltpu.VMEM((2, 2 * N, H), f32),
            pltpu.VMEM((2, 2 * N, H), f32),
            pltpu.VMEM((2, 8, H), f32),
            pltpu.VMEM((H, CG), bf16),
            pltpu.VMEM((H, H * N), bf16),
        ],
        compiler_params=pltpu.CompilerParams(vmem_limit_bytes=60 * 2**20),
        name="ssm",
    )(
        slot_index, tree_sizes, parents, value_stream, gate_stream, key_query_stream, step_stream, caches,
        key_query_cache, value_conv, key_query_conv, bias, rate, skip, norm_gain, cached_state,
    )
    cols = out_weight.shape[1]
    vmem = pl.BlockSpec(memory_space=pltpu.VMEM)
    dma = pltpu.SemaphoreType.DMA
    out = pl.pallas_call(
        functools.partial(comm_kernel, R),
        out_shape=jax.ShapeDtypeStruct((Q, N // 2, R * cols), bf16),
        in_specs=[vmem, vmem, pl.BlockSpec(memory_space=pl.ANY)],
        out_specs=vmem,
        scratch_shapes=[
            pltpu.VMEM(out_weight.shape, bf16),
            pltpu.VMEM((R, G, packed_rows, CG), bf16),
            pltpu.VMEM((R, packed_rows, cols), f32),
            pltpu.VMEM((R, packed_rows, cols), f32),
            pltpu.VMEM((R, packed_rows, cols), bf16),
            pltpu.VMEM((R, packed_rows, cols), bf16),
            dma, dma((3, R, G)), dma((R, G)), dma((R,)), dma((R,)), dma((R,)), dma((R,)),
        ],
        compiler_params=pltpu.CompilerParams(
            collective_id=0, has_side_effects=True, vmem_limit_bytes=60 * 2**20
        ),
        name="project",
    )(packed, unpack, out_weight)
    return (out, final_state)


def solution(mesh):
    return jax.shard_map(
        local,
        mesh=mesh,
        in_specs=(
            P(("group", "req"), None, "chan"),
            P(("group", "req"), None, "chan"),
            P(("group", "req"), None, "chan", None),
            P(("group", "req"), None, "chan"),
            P(("group", "req"), None),
            P(("group", "req")),
            P(("group", "req")),
            P(("group", "req"), None, "chan"),
            P(("group", "req"), None, "chan", None),
            P(None, "chan"),
            P(None, "chan", None),
            P("chan"),
            P("chan"),
            P("chan"),
            P("chan"),
            P(("group", "req"), "chan", None, None),
            P("chan", "req"),
        ),
        out_specs=(P(("group", "req"), "chan", None), P(("group", "req"), "chan", None, None)),
        check_vma=False,
    )
```
